32 devices in a mesh: groups: 2 (over y), dp: 4 (over z), tensor: 4 (over x, core).
Axes of the slice: x: 2, y: 2, z: 4, core: 2. Of those that a mesh axis runs over, the one named last changes fastest.
Arguments:
- queries: bfloat16 [96, 128, 576], P(('groups', 'dp'), 'tensor'), parts along dimension 0, may hold values from -4 to 4
- latent_cache: bfloat16 [96, 128, 576], P(('groups', 'dp')), parts along dimension 0, may hold values from -4 to 4
- lengths: int32 [96], P(('groups', 'dp')), parts along dimension 0, may hold values from 2 to 128, as said below
- value_up: bfloat16 [128, 512, 128], P('tensor'), may hold values from -0.25 to 0.25
- out_proj: bfloat16 [16384, 7168], P('tensor', 'dp'), may hold values from -0.046875 to 0.046875
- residual: bfloat16 [96, 7168], P('groups', 'dp'), parts along dimension 0, may hold values from -1.5 to 1.5
- expert_ids: int32 [96, 8], P('groups'), parts along dimension 0, may hold values from 0 to 255, as said below
- gate_weights: float32 [96, 8], P('groups'), parts along dimension 0, may hold values from 0.1 to 1
- placement: int32 [512], P('groups'), parts along dimension 0, may hold values from 0 to 255, as said below
- norm_gain: bfloat16 [7168], replicated, may hold values from 0.5 to 1.5
- w_gate: bfloat16 [4, 7168, 2048], P('dp', None, 'tensor'), may hold values from -0.0625 to 0.0625
- w_up: bfloat16 [4, 7168, 2048], P('dp', None, 'tensor'), may hold values from -0.0625 to 0.0625
Outputs:
- attn_out: bfloat16 [96, 7168], P('groups', ('dp', 'tensor')), parts along dimension 0
- expert_hidden: bfloat16 [8, 3, 2048], P(('groups', 'dp'), None, 'tensor'), parts along dimension 0
The draws below stay inside these ranges and needn't reach their ends.
There are 2 independent parts, one for each index of `groups`. The reference program is written for one: setup_inputs(seed, part) draws one part's arguments, and reference() takes and returns one part's arrays. A program takes and returns all parts, laid end to end along the dimension named above; an argument that names none is the same for every part. Nothing has to cross between parts.
Inputs may be any that keep to these rules, and one draw needn't show every extreme that they name: `lengths`: in every draw some request has all 128 positions cached. `expert_ids`: each row names 8 different experts. `placement`: a permutation of 0 to 255; in every draw some expert at a position under 4 is named by 3 rows or more.
All inputs are finite; a program needn't handle non-finite values.
Results may differ from the reference program's by a relative error of at most 0.0088.
Values may be sent and summed in bfloat16 or wider, within the bound.
A program may use at most 128 MiB of HBM per device.

```python
import math
import jax
import jax.numpy as jnp
from jax import lax

D = 7168
H = 128
LATENT = 512
ROPE = 64
VHEAD = 128
FF = 2048
EXPERTS = 256
TOPK = 8
CTX = 128
TOKENS = 48
HELD = 4
CAP = 3


def attention_pair(key, strength):
    key = jax.random.fold_in(key, 202)
    total_width = LATENT + ROPE
    key_qn = jax.random.fold_in(key, 0)
    key_cn = jax.random.fold_in(key, 1)
    key_sign = jax.random.fold_in(key, 4)
    query_normal = jnp.clip(jax.random.normal(key_qn, (TOKENS, H, total_width), jnp.float32), -4.0, 4.0)
    cache_normal = jnp.clip(jax.random.normal(key_cn, (TOKENS, CTX, total_width), jnp.float32), -4.0, 4.0)
    queries = query_normal
    caches = cache_normal
    sign_table = jnp.where(jax.random.bernoulli(key_sign, 0.5, (TOKENS, total_width)), 1.0, -1.0)
    request_ids = jnp.arange(TOKENS)
    strength_level = (2 + request_ids // 8 % 3).astype(jnp.float32)
    aligned = (request_ids % 8 == 0).astype(jnp.float32) * strength > 0.5
    columns = jnp.arange(total_width)
    half_width = LATENT // 2
    second_half = (columns >= half_width) & (columns < LATENT)
    zero_count = jnp.where(strength_level < 2.5, 4, 2)
    key_first = 4.0 * sign_table
    key_second = jnp.where(second_half[None, :], -4.0 * sign_table, jnp.where(columns[None, :] < zero_count[:, None], 0.0, 4.0 * sign_table))
    aligned_query = jnp.where(second_half[None, :], 0.0, strength_level[:, None] * sign_table)
    queries = jnp.where(aligned[:, None, None], aligned_query[:, None, :], queries)
    caches = caches.at[:, 0, :].set(jnp.where(aligned[:, None], key_first, caches[:, 0, :]))
    caches = caches.at[:, 1, :].set(jnp.where(aligned[:, None], key_second, caches[:, 1, :]))
    return (queries, caches)


def draw_queries(key, part):
    queries, caches = attention_pair(key, 0.0)
    return queries.astype(jnp.bfloat16)


def draw_latent_cache(key, part):
    queries, caches = attention_pair(key, 0.0)
    return caches.astype(jnp.bfloat16)


def draw_lengths(key, part):
    key = jax.random.fold_in(key, 7)
    key_len, key_full = jax.random.split(key)
    drawn = jax.random.randint(key_len, (TOKENS,), max(2, CTX // 8), CTX + 1)
    full_request = jax.random.randint(key_full, (), 0, TOKENS)
    return jnp.where(jnp.arange(TOKENS) == full_request, CTX, drawn).astype(jnp.int32)


def route_pair(key):
    key = jax.random.fold_in(key, 101)
    key_hot, key_noise, key_forced, key_perm, key_slot = jax.random.split(key, 5)
    hot_score = jax.random.randint(key_hot, (EXPERTS,), 0, 32768)
    noise_score = jax.random.randint(key_noise, (TOKENS, EXPERTS), 0, 65536)
    forced = jax.random.randint(key_forced, (), 0, EXPERTS)
    row_ids = jnp.arange(TOKENS)[:, None]
    column_ids = jnp.arange(EXPERTS)
    boost_score = jnp.where((row_ids < CAP) & (column_ids[None, :] == forced), 1 << 20, 0)
    total_score = (noise_score + hot_score[None, :] + boost_score) * EXPERTS + column_ids[None, :]
    unused, chosen_ids = lax.top_k(total_score, TOPK)
    shuffled = jax.random.permutation(key_perm, EXPERTS).astype(jnp.int32)
    held_slot = jax.random.randint(key_slot, (), 0, HELD)
    forced_pos = jnp.sum(jnp.where(column_ids == forced, shuffled, 0))
    displaced = jnp.argmax(shuffled == held_slot)
    placed = jnp.where(column_ids == forced, held_slot, jnp.where(column_ids == displaced, forced_pos, shuffled))
    return (chosen_ids.astype(jnp.int32), placed.astype(jnp.int32))


def draw_expert_ids(key, part):
    chosen_ids, placed = route_pair(key)
    return chosen_ids


def draw_placement(key, part):
    chosen_ids, placed = route_pair(key)
    return placed


def level_of(own_key, dims, pieces, smallest, top_value):
    factor_of, own = 1.0, jax.random.fold_in(own_key, 6)
    for dim, shards_of in pieces:
        steps = jnp.exp(jax.random.uniform(jax.random.fold_in(own, dim), (shards_of,), jnp.float32, smallest / len(pieces), top_value / len(pieces)))
        factor_of = factor_of * jnp.repeat(steps, dims[dim] // shards_of).reshape([-1 if axis == dim else 1 for axis in range(len(dims))])
    return factor_of


def noise(own_key, shape, deviation, bound, cuts=(), kind=jnp.bfloat16):
    result = deviation * jax.random.normal(own_key, shape, jnp.float32)
    if cuts:
        result = result * level_of(own_key, shape, cuts, -0.22, 0.18)
    return jnp.clip(result, -bound, bound).astype(kind)


def setup_inputs(seed: int = 0, part: int = 0) -> dict:
    key_of = jax.random.split(jax.random.key(seed), 13)
    own_keys = jax.random.split(jax.random.fold_in(key_of[12], part), 13)
    return {
        "queries": draw_queries(jax.random.fold_in(jax.random.fold_in(key_of[12], part), 71), part),
        "latent_cache": draw_latent_cache(jax.random.fold_in(jax.random.fold_in(key_of[12], part), 71), part),
        "lengths": draw_lengths(jax.random.fold_in(jax.random.fold_in(key_of[12], part), 71), part),
        "value_up": noise(key_of[3], (H, LATENT, VHEAD), LATENT ** -0.5, 0.25, ((0, 4),)),
        "out_proj": noise(key_of[4], (H * VHEAD, D), (H * VHEAD) ** -0.5, 0.046875, ((0, 4), (1, 4))),
        "residual": noise(own_keys[5], (TOKENS, D), 0.25, 1.5, ((1, 4),)),
        "expert_ids": draw_expert_ids(jax.random.fold_in(jax.random.fold_in(key_of[12], part), 71), part),
        "gate_weights": jnp.clip(jnp.exp(jax.random.uniform(own_keys[7], (TOKENS, TOPK), jnp.float32, math.log(0.1), math.log(1.0))), 0.1, 1.0),
        "placement": draw_placement(jax.random.fold_in(jax.random.fold_in(key_of[12], part), 71), part),
        "norm_gain": jnp.clip(1.0 + 0.1 * jax.random.normal(key_of[9], (D,), jnp.float32), 0.5, 1.5).astype(jnp.bfloat16),
        "w_gate": noise(key_of[10], (HELD, D, FF), D ** -0.5, 0.0625, ((0, 4), (2, 4))),
        "w_up": noise(key_of[11], (HELD, D, FF), D ** -0.5, 0.0625, ((0, 4), (2, 4))),
    }


def slot_table(expert_ids, placement):
    flat_ids = expert_ids.reshape(-1)
    id_match = flat_ids[:, None] == jnp.arange(EXPERTS, dtype=jnp.int32)[None, :]
    position = lax.optimization_barrier(jnp.sum(jnp.where(id_match, placement[None, :], 0), axis=1)).astype(jnp.int32)
    chosen = (position[:, None] == jnp.arange(HELD, dtype=jnp.int32)[None, :]).astype(jnp.int32)
    earlier = jnp.cumsum(chosen, axis=0) - chosen
    slot_index = lax.optimization_barrier(jnp.sum(chosen * earlier, axis=1)).astype(jnp.int32)
    kept_slot = (position < HELD) & (slot_index < CAP)
    target = jnp.where(kept_slot, position * CAP + slot_index, HELD * CAP).astype(jnp.int32)
    return target.reshape(TOKENS, TOPK)

def reference(queries, latent_cache, lengths, value_up, out_proj, residual, expert_ids, gate_weights, placement, norm_gain, w_gate, w_up):
    score_scale = (VHEAD + ROPE) ** (-0.5)
    scores = jnp.einsum('thc,tsc->ths', queries.astype(jnp.float32), latent_cache.astype(jnp.float32)) * score_scale
    live_keys = jnp.arange(CTX, dtype=jnp.int32)[None, None, :] < lengths[:, None, None]
    scores = jnp.where(live_keys, scores, -jnp.inf)
    row_max = lax.optimization_barrier(jnp.max(scores, axis=2, keepdims=True))
    exponent = jnp.exp(scores - row_max)
    attention_weights = (exponent / lax.optimization_barrier(jnp.sum(exponent, axis=2, keepdims=True))).astype(jnp.bfloat16)
    context = jnp.einsum('ths,tsc->thc', attention_weights.astype(jnp.float32), latent_cache[:, :, :LATENT].astype(jnp.float32)).astype(jnp.bfloat16)
    head_out = jnp.einsum('thc,hcv->thv', context.astype(jnp.float32), value_up.astype(jnp.float32)).astype(jnp.bfloat16)
    projected = jnp.dot(head_out.reshape(TOKENS, H * VHEAD), out_proj, preferred_element_type=jnp.float32)
    attn_out = (projected + residual.astype(jnp.float32)).astype(jnp.bfloat16)
    target = slot_table(expert_ids, placement)
    slot_ids = jnp.arange(HELD * CAP, dtype=jnp.int32)
    slot_match = target[:, :, None] == slot_ids[None, None, :]
    onehot = jnp.any(slot_match, axis=1).astype(jnp.bfloat16)
    expert_rows = jnp.dot(onehot.T, attn_out, preferred_element_type=jnp.float32).astype(jnp.bfloat16).reshape(HELD, CAP, D)
    slot_gate = lax.optimization_barrier(jnp.sum(jnp.where(slot_match, gate_weights[:, :, None], 0.0), axis=(0, 1))).reshape(HELD, CAP)

    def expert_step(packed):
        slot_rows, gate_mat, up_mat, gates = packed
        values = slot_rows.astype(jnp.float32)
        mean_square = lax.optimization_barrier(jnp.mean(values * values, axis=-1, keepdims=True))
        normed = (values * lax.rsqrt(mean_square + 1e-06) * norm_gain.astype(jnp.float32)).astype(jnp.bfloat16)
        gate_proj = jnp.dot(normed, gate_mat, preferred_element_type=jnp.float32)
        up_proj = jnp.dot(normed, up_mat, preferred_element_type=jnp.float32)
        return (gates[:, None] * jax.nn.silu(gate_proj) * up_proj).astype(jnp.bfloat16)
    expert_hidden = lax.map(expert_step, (expert_rows, w_gate, w_up, slot_gate))
    return (attn_out, expert_hidden)
```

```python
import functools

import jax
import jax.numpy as jnp
from jax import lax
from jax.experimental import pallas as pl
from jax.experimental.pallas import tpu as pltpu
from jax.sharding import PartitionSpec as P

LATENT = 512
ROPE = 64
VHEAD = 128
EXPERTS = 256
TOPK = 8
F32 = jnp.float32
BF16 = jnp.bfloat16
MESH = pl.DeviceIdType.MESH


def layer_kernel(
    dp_count,
    tp_count,
    q_hbm,
    cache_hbm,
    len_ref,
    vu_hbm,
    wo_hbm,
    res_ref,
    ids_ref,
    gates_ref,
    place_ref,
    gain_ref,
    wg_hbm,
    wu_hbm,
    attn_ref,
    hid_ref,
    q_s,
    cache_s,
    vu_s,
    wo_s,
    wg_s,
    wu_s,
    ctx_s,
    hbuf,
    acc_s,
    stg,
    own_s,
    red_send,
    red_recv,
    onehot_s,
    disp,
    xrecv,
    sg_s,
    in_sem,
    vu_sem,
    wo_sem,
    we_sem,
    ag_send,
    ag_recv,
    rs_send,
    rs_recv,
    dx_send,
    dx_recv,
):
    g = lax.axis_index("groups")
    d = lax.axis_index("dp")
    t = lax.axis_index("tensor")
    peers = dp_count * tp_count
    me = d * tp_count + t
    tokens, heads, width = q_s.shape
    rows_pad = ctx_s.shape[1] // heads
    chunks = hbuf.shape[0]
    hpc = heads // chunks
    kc = hpc * VHEAD
    cols = attn_ref.shape[1]
    pad = own_s.shape[2]
    all_tokens = attn_ref.shape[0]
    model = wg_hbm.shape[1]
    ff = wg_hbm.shape[2]
    capacity = hid_ref.shape[1]

    q_copy = pltpu.make_async_copy(q_hbm, q_s, in_sem.at[0])
    c_copy = pltpu.make_async_copy(cache_hbm, cache_s, in_sem.at[1])
    q_copy.start()
    c_copy.start()

    barrier = pltpu.get_barrier_semaphore()
    for o in range(1, peers):
        other = lax.rem(me + o, peers)
        pl.semaphore_signal(
            barrier,
            inc=1,
            device_id=(g, other // tp_count, lax.rem(other, tp_count)),
            device_id_type=MESH,
        )

    vu_copies = [
        pltpu.make_async_copy(
            vu_hbm.at[pl.ds(c * hpc, hpc)], vu_s.at[pl.ds(c * hpc, hpc)], vu_sem.at[c]
        )
        for c in range(chunks)
    ]
    wo_copies = [
        pltpu.make_async_copy(
            wo_hbm.at[pl.ds(c * kc, kc)], wo_s.at[pl.ds(c * kc, kc)], wo_sem.at[c]
        )
        for c in range(chunks)
    ]
    wg_copy = pltpu.make_async_copy(wg_hbm.at[0], wg_s.at[pl.ds(0, model)], we_sem.at[0])
    wu_copy = pltpu.make_async_copy(wu_hbm.at[0], wu_s.at[pl.ds(0, model)], we_sem.at[1])
    for cp in vu_copies:
        cp.start()

    ids = ids_ref[...]
    gates = gates_ref[...]
    place = place_ref[...]
    expert_iota = lax.broadcasted_iota(jnp.int32, place.shape, 1)

    def choice(position):
        expert = jnp.sum(jnp.where(place == position, expert_iota, 0), axis=1, keepdims=True)
        return ids == expert

    row8 = lax.broadcasted_iota(jnp.int32, (8, all_tokens), 0)
    match = jnp.zeros((8, all_tokens), F32)
    for p in range(dp_count):
        hit = jnp.sum(choice(p).astype(F32), axis=0, keepdims=True)
        match = jnp.where(row8 == p, hit, match)
    own_choice = choice(d)
    own_hit = jnp.sum(own_choice.astype(F32), axis=0, keepdims=True)
    own_gate = jnp.sum(jnp.where(own_choice, gates, 0.0), axis=0, keepdims=True)
    match = jnp.where(row8 == dp_count, own_hit, match)
    up_r = lax.broadcasted_iota(jnp.int32, (all_tokens, all_tokens), 0)
    up_c = lax.broadcasted_iota(jnp.int32, (all_tokens, all_tokens), 1)
    upper = jnp.where(up_r < up_c, 1.0, 0.0).astype(BF16)
    earlier = jnp.dot(match.astype(BF16), upper, preferred_element_type=F32)
    shape = (16 * dp_count, all_tokens)
    rep_m = jnp.concatenate(
        [jnp.broadcast_to(match[p : p + 1], (16, all_tokens)) for p in range(dp_count)], axis=0
    )
    rep_e = jnp.concatenate(
        [jnp.broadcast_to(earlier[p : p + 1], (16, all_tokens)) for p in range(dp_count)], axis=0
    )
    r_iota = lax.broadcasted_iota(jnp.int32, shape, 0)
    slot = r_iota & 3
    quarter = (r_iota >> 2) & 3
    kept = jnp.where((rep_e == slot.astype(F32)) & (slot < capacity), rep_m, 0.0)
    for q in range(4):
        onehot_s[q] = jnp.where(quarter == q, kept, 0.0).astype(BF16)
    own_e = jnp.broadcast_to(earlier[dp_count : dp_count + 1], (8, all_tokens))
    own_g = jnp.broadcast_to(own_gate * own_hit, (8, all_tokens))
    sg_s[...] = jnp.broadcast_to(
        jnp.sum(
            jnp.where((own_e == row8.astype(F32)) & (row8 < capacity), own_g, 0.0),
            axis=1,
            keepdims=True,
        ),
        sg_s.shape,
    )

    ctx_s[...] = jnp.zeros_like(ctx_s)
    wg_s[pl.ds(model, wg_s.shape[0] - model), :] = jnp.zeros((wg_s.shape[0] - model, ff), BF16)
    wu_s[pl.ds(model, wu_s.shape[0] - model), :] = jnp.zeros((wu_s.shape[0] - model, ff), BF16)
    stg[:, pl.ds(tp_count * cols, stg.shape[1] - tp_count * cols)] = jnp.zeros(
        (all_tokens, stg.shape[1] - tp_count * cols), F32
    )

    q_copy.wait()
    c_copy.wait()
    for cp in wo_copies:
        cp.start()
    wg_copy.start()
    wu_copy.start()

    score_scale = (VHEAD + ROPE) ** (-0.5)
    ctx_len = cache_s.shape[2]

    def token_step(i, carry):
        scores = jnp.dot(q_s[i], cache_s[i], preferred_element_type=F32) * score_scale
        live = lax.broadcasted_iota(jnp.int32, (heads, ctx_len), 1) < len_ref[i]
        scores = jnp.where(live, scores, -jnp.inf)
        top = jnp.max(scores, axis=1, keepdims=True)
        e = jnp.exp(scores - top)
        w = (e / jnp.sum(e, axis=1, keepdims=True)).astype(BF16)
        context = lax.dot_general(
            w,
            cache_s[i, pl.ds(0, LATENT), :],
            (((1,), (1,)), ((), ())),
            preferred_element_type=F32,
        )
        for k in range(LATENT // 128):
            ctx_s[k, pl.ds(i, heads, stride=rows_pad), :] = context[:, k * 128 : (k + 1) * 128]
        return carry

    lax.fori_loop(0, tokens, token_step, 0, unroll=UNROLL)

    def ag_copy(c, o):
        peer = lax.rem(d + o, dp_count)
        return pltpu.make_async_remote_copy(
            src_ref=hbuf.at[c, d],
            dst_ref=hbuf.at[c, d],
            send_sem=ag_send.at[c, o],
            recv_sem=ag_recv.at[c, d],
            device_id=(g, peer, t),
            device_id_type=MESH,
        )

    def ag_arrival(c, o):
        src = lax.rem(d + o, dp_count)
        return pltpu.make_async_remote_copy(
            src_ref=hbuf.at[c, src],
            dst_ref=hbuf.at[c, src],
            send_sem=ag_send.at[c, o],
            recv_sem=ag_recv.at[c, src],
            device_id=(g, src, t),
            device_id_type=MESH,
        )

    for c in range(chunks):
        vu_copies[c].wait()
        for hl in range(hpc):
            h = c * hpc + hl
            rows = jnp.concatenate(
                [ctx_s[k, pl.ds(h * rows_pad, rows_pad), :] for k in range(LATENT // 128)], axis=1
            ).astype(BF16)
            out = jnp.dot(rows, vu_s[h], preferred_element_type=F32)
            hbuf[c, d, :, pl.ds(hl * VHEAD, VHEAD)] = out.astype(BF16)
        if c == 0:
            pl.semaphore_wait(barrier, peers - 1)
        for o in range(1, dp_count):
            ag_copy(c, o).start()

    acc_s[...] = jnp.zeros_like(acc_s)
    n_tile = 256
    n_count = wo_s.shape[1] // n_tile
    for c in range(chunks):
        wo_copies[c].wait()
        for o in range(1, dp_count):
            ag_arrival(c, o).wait_recv()
        left = hbuf[c].reshape(dp_count * rows_pad, kc)

        def n_step(n, carry, c=c, left=left):
            sl = pl.ds(pl.multiple_of(n * n_tile, n_tile), n_tile)
            acc_s[:, sl] += jnp.dot(
                left, wo_s[pl.ds(c * kc, kc), sl], preferred_element_type=F32
            )
            return carry

        lax.fori_loop(0, n_count, n_step, 0, unroll=True)

    for k in range(dp_count):
        stg[pl.ds(k * tokens, tokens), pl.ds(0, tp_count * cols)] = acc_s[
            pl.ds(k * rows_pad, tokens), :
        ]

    lane = lax.broadcasted_iota(jnp.int32, (all_tokens, pad), 1)
    for j in range(tp_count):
        piece = jnp.where(lane < cols, stg[:, pl.ds(j * cols, pad)], 0.0)
        red_send[j] = piece.astype(BF16)
        own_s[j] = piece

    def rs_copy(o):
        peer = lax.rem(t + o, tp_count)
        return pltpu.make_async_remote_copy(
            src_ref=red_send.at[peer],
            dst_ref=red_recv.at[t],
            send_sem=rs_send.at[o],
            recv_sem=rs_recv.at[t],
            device_id=(g, d, peer),
            device_id_type=MESH,
        )

    def rs_arrival(o):
        src = lax.rem(t + o, tp_count)
        return pltpu.make_async_remote_copy(
            src_ref=red_send.at[src],
            dst_ref=red_recv.at[src],
            send_sem=rs_send.at[o],
            recv_sem=rs_recv.at[src],
            device_id=(g, d, src),
            device_id_type=MESH,
        )

    for o in range(1, tp_count):
        rs_copy(o).start()
    total = own_s[t] + res_ref[t].astype(F32)
    for o in range(1, tp_count):
        rs_arrival(o).wait_recv()
        total = total + red_recv[lax.rem(t + o, tp_count)].astype(F32)
    stream = total.astype(BF16)
    attn_ref[...] = stream[:, :cols]

    packed = jnp.zeros((16 * dp_count, 128), F32)
    for q in range(4):
        packed = packed + jnp.dot(
            onehot_s[q], stream[:, q * 128 : (q + 1) * 128], preferred_element_type=F32
        )
    packed = packed.astype(BF16)
    for p in range(dp_count):
        disp[p] = packed[p * 16 : (p + 1) * 16]

    def dx_copy(o):
        other = lax.rem(me + o, peers)
        return pltpu.make_async_remote_copy(
            src_ref=disp.at[other // tp_count],
            dst_ref=xrecv.at[me],
            send_sem=dx_send.at[o],
            recv_sem=dx_recv.at[me],
            device_id=(g, other // tp_count, lax.rem(other, tp_count)),
            device_id_type=MESH,
        )

    def dx_arrival(o):
        src = lax.rem(me + o, peers)
        return pltpu.make_async_remote_copy(
            src_ref=disp.at[0],
            dst_ref=xrecv.at[src],
            send_sem=dx_send.at[o],
            recv_sem=dx_recv.at[src],
            device_id=(g, src // tp_count, lax.rem(src, tp_count)),
            device_id_type=MESH,
        )

    for o in range(1, peers):
        dx_copy(o).start()
    xrecv[me] = disp[d]
    wg_copy.wait()
    wu_copy.wait()

    group = lax.broadcasted_iota(jnp.int32, (16, 128), 0) >> 2
    acc_g = jnp.zeros((16, ff), F32)
    acc_u = jnp.zeros((16, ff), F32)
    squares = jnp.zeros((16, 128), F32)

    def expert_piece(src, carry):
        acc_g, acc_u, squares = carry
        values = xrecv[src].astype(F32)
        scaled = values * gain_ref[src].astype(F32)
        left = jnp.concatenate(
            [jnp.where(group == q, scaled, 0.0) for q in range(4)], axis=1
        ).astype(BF16)
        sl = pl.ds(pl.multiple_of(src * cols, 64), pad)
        acc_g = acc_g + jnp.dot(left, wg_s[sl, :], preferred_element_type=F32)
        acc_u = acc_u + jnp.dot(left, wu_s[sl, :], preferred_element_type=F32)
        return acc_g, acc_u, squares + values * values

    carry = expert_piece(me, (acc_g, acc_u, squares))

    def expert_step(o, carry):
        dx_arrival(o).wait_recv()
        return expert_piece(lax.rem(me + o, peers), carry)

    acc_g, acc_u, squares = lax.fori_loop(1, peers, expert_step, carry)

    def fold(a):
        return a[0:4] + a[4:8] + a[8:12] + a[12:16]

    mean_square = fold(jnp.sum(squares, axis=1, keepdims=True)) / model
    scale = lax.rsqrt(mean_square + 1e-06)
    gate_proj = fold(acc_g) * scale
    up_proj = fold(acc_u) * scale
    hidden = sg_s[0:4, 0:1] * (gate_proj / (1.0 + jnp.exp(-gate_proj))) * up_proj
    hid_ref[0] = hidden[0:capacity].astype(BF16)

    for c in range(chunks):
        for o in range(1, dp_count):
            ag_copy(c, o).wait_send()
    for o in range(1, tp_count):
        rs_copy(o).wait_send()
    for o in range(1, peers):
        dx_copy(o).wait_send()


UNROLL = 2


def fused_layer(
    queries,
    latent_cache,
    lengths,
    value_up,
    out_proj,
    residual,
    expert_ids,
    gate_weights,
    placement,
    norm_gain,
    w_gate,
    w_up,
):
    dp_count = lax.axis_size("dp")
    tp_count = lax.axis_size("tensor")
    all_tokens = expert_ids.shape[0]
    capacity = max(2, all_tokens * TOPK * 2 // EXPERTS)
    tokens, heads, width = queries.shape
    cols = residual.shape[1] // tp_count
    model = norm_gain.shape[0]
    ff = w_gate.shape[2]
    pad = 512
    chunks = 4
    rows_pad = 16
    peers = dp_count * tp_count
    hpc = heads // chunks
    gain = jnp.pad(norm_gain.reshape(peers, cols), ((0, 0), (0, pad - cols)))
    gain = jnp.broadcast_to(gain.reshape(peers, 4, 1, 128), (peers, 4, 4, 128)).reshape(
        peers, 16, 128
    )
    res = jnp.pad(
        residual.reshape(all_tokens, tp_count, cols).transpose(1, 0, 2),
        ((0, 0), (0, 0), (0, pad - cols)),
    )
    hbm = pl.BlockSpec(memory_space=pl.ANY)
    vmem = pl.BlockSpec(memory_space=pltpu.VMEM)
    smem = pl.BlockSpec(memory_space=pltpu.SMEM)
    dma = pltpu.SemaphoreType.DMA
    return pl.pallas_call(
        functools.partial(layer_kernel, dp_count, tp_count),
        out_shape=(
            jax.ShapeDtypeStruct((all_tokens, cols), BF16),
            jax.ShapeDtypeStruct((1, capacity, ff), BF16),
        ),
        in_specs=[hbm, hbm, smem, hbm, hbm, vmem, vmem, vmem, vmem, vmem, hbm, hbm],
        out_specs=(vmem, vmem),
        scratch_shapes=[
            pltpu.VMEM((tokens, heads, width), BF16),
            pltpu.VMEM((tokens, width, latent_cache.shape[1]), BF16),
            pltpu.VMEM(value_up.shape, BF16),
            pltpu.VMEM(out_proj.shape, BF16),
            pltpu.VMEM((model + pad - cols, ff), BF16),
            pltpu.VMEM((model + pad - cols, ff), BF16),
            pltpu.VMEM((LATENT // 128, heads * rows_pad, 128), F32),
            pltpu.VMEM((chunks, dp_count, rows_pad, hpc * VHEAD), BF16),
            pltpu.VMEM((dp_count * rows_pad, tp_count * cols), F32),
            pltpu.VMEM((all_tokens, tp_count * cols + 128), F32),
            pltpu.VMEM((tp_count, all_tokens, pad), F32),
            pltpu.VMEM((tp_count, all_tokens, pad), BF16),
            pltpu.VMEM((tp_count, all_tokens, pad), BF16),
            pltpu.VMEM((4, 16 * dp_count, all_tokens), BF16),
            pltpu.VMEM((dp_count, 16, 128), BF16),
            pltpu.VMEM((peers, 16, 128), BF16),
            pltpu.VMEM((8, 128), F32),
            dma((2,)),
            dma((chunks,)),
            dma((chunks,)),
            dma((2,)),
            dma((chunks, dp_count)),
            dma((chunks, dp_count)),
            dma((tp_count,)),
            dma((tp_count,)),
            dma((peers,)),
            dma((peers,)),
        ],
        compiler_params=pltpu.CompilerParams(
            collective_id=0, has_side_effects=True, vmem_limit_bytes=58 * 1024 * 1024
        ),
    )(
        queries,
        jnp.swapaxes(latent_cache, 1, 2),
        lengths,
        value_up,
        out_proj,
        res,
        expert_ids.T,
        gate_weights.T,
        placement.reshape(1, -1),
        gain,
        w_gate,
        w_up,
    )


def slot_table(expert_ids, placement, held_count, capacity):
    flat_ids = expert_ids.reshape(-1)
    id_match = flat_ids[:, None] == jnp.arange(EXPERTS, dtype=jnp.int32)[None, :]
    position = jnp.sum(jnp.where(id_match, placement[None, :], 0), axis=1)
    chosen = (position[:, None] == jnp.arange(held_count, dtype=jnp.int32)[None, :]).astype(
        jnp.int32
    )
    earlier = jnp.cumsum(chosen, axis=0) - chosen
    slot_index = jnp.sum(chosen * earlier, axis=1)
    kept_slot = (position < held_count) & (slot_index < capacity)
    target = jnp.where(kept_slot, position * capacity + slot_index, held_count * capacity)
    return target.reshape(expert_ids.shape)


def on_device(
    queries,
    latent_cache,
    lengths,
    value_up,
    out_proj,
    residual,
    expert_ids,
    gate_weights,
    placement,
    norm_gain,
    w_gate,
    w_up,
):
    dp_count = lax.axis_size("dp")
    tensor_count = lax.axis_size("tensor")
    token_count = expert_ids.shape[0]
    local_experts = w_gate.shape[0]
    held_count = local_experts * dp_count
    capacity = max(2, token_count * TOPK * 2 // EXPERTS)
    score_scale = (VHEAD + ROPE) ** (-0.5)
    scores = (
        jnp.einsum("thc,tsc->ths", queries, latent_cache, preferred_element_type=jnp.float32)
        * score_scale
    )
    live_keys = (
        jnp.arange(latent_cache.shape[1], dtype=jnp.int32)[None, None, :] < lengths[:, None, None]
    )
    scores = jnp.where(live_keys, scores, -jnp.inf)
    row_max = jnp.max(scores, axis=2, keepdims=True)
    exponent = jnp.exp(scores - row_max)
    attention_weights = (exponent / jnp.sum(exponent, axis=2, keepdims=True)).astype(jnp.bfloat16)
    context = jnp.einsum(
        "ths,tsc->thc",
        attention_weights,
        latent_cache[:, :, :LATENT],
        preferred_element_type=jnp.float32,
    ).astype(jnp.bfloat16)
    head_out = jnp.einsum(
        "thc,hcv->thv", context, value_up, preferred_element_type=jnp.float32
    ).astype(jnp.bfloat16)
    head_out = head_out.reshape(head_out.shape[0], -1)
    partial_sum = jnp.dot(
        lax.all_gather(head_out, "dp", axis=0, tiled=True),
        out_proj,
        preferred_element_type=jnp.float32,
    )
    target = slot_table(expert_ids, placement, held_count, capacity)
    slot_ids = jnp.arange(held_count * capacity, dtype=jnp.int32)
    slot_match = target[:, :, None] == slot_ids[None, None, :]
    onehot = jnp.any(slot_match, axis=1).astype(jnp.bfloat16)
    gate_all = jnp.sum(jnp.where(slot_match, gate_weights[:, :, None], 0.0), axis=(0, 1))
    owner_span = local_experts * capacity
    owner_index = lax.axis_index("dp")
    slot_gate = lax.dynamic_slice_in_dim(gate_all, owner_index * owner_span, owner_span).reshape(
        local_experts, capacity
    )
    gain_values = norm_gain.astype(jnp.float32)
    tensor_pos = lax.axis_index("tensor")
    summed_all = lax.psum(partial_sum, "tensor")
    stream_cols = (summed_all + residual.astype(jnp.float32)).astype(jnp.bfloat16)
    col_width = stream_cols.shape[1] // tensor_count
    attn_out = lax.dynamic_slice_in_dim(stream_cols, tensor_pos * col_width, col_width, 1)
    buffer = jnp.einsum(
        "td,tc->dc", onehot, stream_cols, preferred_element_type=jnp.float32
    ).astype(jnp.bfloat16)
    buffer = buffer.reshape(held_count, capacity, -1)
    values = lax.all_to_all(buffer, "dp", split_axis=0, concat_axis=2, tiled=True).astype(
        jnp.float32
    )
    mean_square = jnp.mean(values * values, axis=-1, keepdims=True)
    normed = (values * lax.rsqrt(mean_square + 1e-06) * gain_values).astype(jnp.bfloat16)
    gate_proj = jnp.einsum("end,edf->enf", normed, w_gate, preferred_element_type=jnp.float32)
    up_proj = jnp.einsum("end,edf->enf", normed, w_up, preferred_element_type=jnp.float32)
    hidden = jax.nn.silu(gate_proj) * up_proj
    result = (slot_gate[:, :, None] * hidden).astype(jnp.bfloat16)
    return (attn_out, result)


def solution(mesh):
    in_specs = (
        P(("groups", "dp"), "tensor", None),
        P(("groups", "dp"), None, None),
        P(("groups", "dp")),
        P("tensor", None, None),
        P("tensor", "dp"),
        P("groups", "dp"),
        P("groups", None),
        P("groups", None),
        P("groups"),
        P(),
        P("dp", None, "tensor"),
        P("dp", None, "tensor"),
    )
    out_specs = (P("groups", ("dp", "tensor")), P(("groups", "dp"), None, "tensor"))

    def layer(*args):
        token_count = args[6].shape[0]
        capacity = max(2, token_count * TOPK * 2 // EXPERTS)
        cols = args[5].shape[1] // mesh.shape["tensor"]
        fits = (
            args[10].shape[0] == 1
            and capacity <= 4
            and 384 < cols <= 512
            and cols % 64 == 0
            and args[5].shape[1] % 256 == 0
            and args[0].shape[0] <= 16
            and args[0].shape[1] % 4 == 0
            and mesh.shape["dp"] < 8
            and token_count % 16 == 0
        )
        return (fused_layer if fits else on_device)(*args)

    return jax.shard_map(
        layer, mesh=mesh, in_specs=in_specs, out_specs=out_specs, check_vma=False
    )
```

```python
import functools

import jax
import jax.numpy as jnp
from jax import lax
from jax.experimental import pallas as pl
from jax.experimental.pallas import tpu as pltpu
from jax.sharding import PartitionSpec as P

LATENT = 512
ROPE = 64
VHEAD = 128
EXPERTS = 256
TOPK = 8
F32 = jnp.float32
BF16 = jnp.bfloat16
MESH = pl.DeviceIdType.MESH


def layer_kernel(
    dp_count,
    tp_count,
    q_hbm,
    cache_hbm,
    len_ref,
    vu_hbm,
    wo_hbm,
    res_ref,
    ids_ref,
    gates_ref,
    place_ref,
    gain_ref,
    wg_hbm,
    wu_hbm,
    attn_ref,
    hid_ref,
    q_s,
    cache_s,
    vu_s,
    wo_s,
    wg_s,
    wu_s,
    ctx_s,
    hbuf,
    pack_s,
    lhs_s,
    gain_a,
    gain_s,
    stg,
    own_s,
    red_send,
    red_recv,
    onehot_s,
    disp,
    xrecv,
    sg_s,
    in_sem,
    vu_sem,
    wo_sem,
    we_sem,
    ag_send,
    ag_recv,
    rs_send,
    rs_recv,
    dx_send,
    dx_recv,
):
    g = lax.axis_index("groups")
    d = lax.axis_index("dp")
    t = lax.axis_index("tensor")
    peers = dp_count * tp_count
    me = d * tp_count + t
    tokens, heads, width = q_s.shape
    rows_pad = ctx_s.shape[1] // heads
    chunks = hbuf.shape[0]
    hpc = heads // chunks
    kc = hpc * VHEAD
    cols = attn_ref.shape[1]
    pad = own_s.shape[2]
    all_tokens = attn_ref.shape[0]
    model = wg_hbm.shape[1]
    ff = wg_hbm.shape[2]
    capacity = hid_ref.shape[1]

    q_copy = pltpu.make_async_copy(q_hbm, q_s, in_sem.at[0])
    c_copy = pltpu.make_async_copy(cache_hbm, cache_s, in_sem.at[1])
    q_copy.start()
    c_copy.start()

    barrier = pltpu.get_barrier_semaphore()
    for o in range(1, peers):
        other = lax.rem(me + o, peers)
        pl.semaphore_signal(
            barrier,
            inc=1,
            device_id=(g, other // tp_count, lax.rem(other, tp_count)),
            device_id_type=MESH,
        )

    vu_copies = [
        pltpu.make_async_copy(
            vu_hbm.at[pl.ds(c * hpc, hpc)], vu_s.at[pl.ds(c * hpc, hpc)], vu_sem.at[c]
        )
        for c in range(chunks)
    ]
    wo_copies = [
        pltpu.make_async_copy(
            wo_hbm.at[pl.ds(c * kc, kc)], wo_s.at[pl.ds(c * kc, kc)], wo_sem.at[c]
        )
        for c in range(chunks)
    ]
    wg_copy = pltpu.make_async_copy(wg_hbm.at[0], wg_s.at[pl.ds(0, model)], we_sem.at[0])
    wu_copy = pltpu.make_async_copy(wu_hbm.at[0], wu_s.at[pl.ds(0, model)], we_sem.at[1])
    for cp in vu_copies:
        cp.start()

    ids = ids_ref[...]
    gates = gates_ref[...]
    place = place_ref[...]
    expert_iota = lax.broadcasted_iota(jnp.int32, place.shape, 1)

    def choice(position):
        expert = jnp.sum(jnp.where(place == position, expert_iota, 0), axis=1, keepdims=True)
        return ids == expert

    row8 = lax.broadcasted_iota(jnp.int32, (8, all_tokens), 0)
    match = jnp.zeros((8, all_tokens), F32)
    for p in range(dp_count):
        hit = jnp.sum(choice(p).astype(F32), axis=0, keepdims=True)
        match = jnp.where(row8 == p, hit, match)
    own_choice = choice(d)
    own_hit = jnp.sum(own_choice.astype(F32), axis=0, keepdims=True)
    own_gate = jnp.sum(jnp.where(own_choice, gates, 0.0), axis=0, keepdims=True)
    match = jnp.where(row8 == dp_count, own_hit, match)
    up_r = lax.broadcasted_iota(jnp.int32, (all_tokens, all_tokens), 0)
    up_c = lax.broadcasted_iota(jnp.int32, (all_tokens, all_tokens), 1)
    upper = jnp.where(up_r < up_c, 1.0, 0.0).astype(BF16)
    earlier = jnp.dot(match.astype(BF16), upper, preferred_element_type=F32)
    shape = (16 * dp_count, all_tokens)
    rep_m = jnp.concatenate(
        [jnp.broadcast_to(match[p : p + 1], (16, all_tokens)) for p in range(dp_count)], axis=0
    )
    rep_e = jnp.concatenate(
        [jnp.broadcast_to(earlier[p : p + 1], (16, all_tokens)) for p in range(dp_count)], axis=0
    )
    r_iota = lax.broadcasted_iota(jnp.int32, shape, 0)
    slot = r_iota & 3
    quarter = (r_iota >> 2) & 3
    kept = jnp.where((rep_e == slot.astype(F32)) & (slot < capacity), rep_m, 0.0)
    for q in range(4):
        onehot_s[q] = jnp.where(quarter == q, kept, 0.0).astype(BF16)
    own_e = jnp.broadcast_to(earlier[dp_count : dp_count + 1], (8, all_tokens))
    own_g = jnp.broadcast_to(own_gate * own_hit, (8, all_tokens))
    sg_s[...] = jnp.broadcast_to(
        jnp.sum(
            jnp.where((own_e == row8.astype(F32)) & (row8 < capacity), own_g, 0.0),
            axis=1,
            keepdims=True,
        ),
        sg_s.shape,
    )

    ctx_s[...] = jnp.zeros_like(ctx_s)
    wg_s[pl.ds(model, wg_s.shape[0] - model), :] = jnp.zeros((wg_s.shape[0] - model, ff), BF16)
    wu_s[pl.ds(model, wu_s.shape[0] - model), :] = jnp.zeros((wu_s.shape[0] - model, ff), BF16)
    total_cols = tp_count * cols
    stg[:, pl.ds(total_cols, stg.shape[1] - total_cols)] = jnp.zeros(
        (all_tokens, stg.shape[1] - total_cols), F32
    )
    stg[:, pl.ds(0, total_cols)] = res_ref[...].astype(F32)
    lane = lax.broadcasted_iota(jnp.int32, (all_tokens, pad), 1)
    for j in range(tp_count):
        own_s[j] = jnp.where(lane < cols, stg[:, pl.ds(j * cols, pad)], 0.0)

    gain_rows = gain_ref.shape[0]
    gain_a[pl.ds(0, gain_rows), :] = gain_ref[...].astype(F32)
    gain_a[pl.ds(gain_rows, 8), :] = jnp.zeros((8, 128), F32)
    half = lax.broadcasted_iota(jnp.int32, (1, 128), 1) >= 64
    group = lax.broadcasted_iota(jnp.int32, (16, 128), 0) >> 2
    for src in range(peers):
        first, odd = divmod(src * cols, 128)
        block = jnp.zeros((16, 128), F32)
        for q in range(4):
            row = gain_a[pl.ds(first + q, 1), :]
            if odd:
                row = pltpu.roll(jnp.where(half, row, gain_a[pl.ds(first + q + 1, 1), :]), 64, 1)
            block = jnp.where(group == q, row, block)
        gain_s[src] = block

    q_copy.wait()
    c_copy.wait()
    for cp in wo_copies:
        cp.start()
    wg_copy.start()
    wu_copy.start()

    score_scale = (VHEAD + ROPE) ** (-0.5)
    ctx_len = cache_s.shape[2]

    def token_step(i, carry):
        scores = jnp.dot(q_s[i], cache_s[i], preferred_element_type=F32) * score_scale
        live = lax.broadcasted_iota(jnp.int32, (heads, ctx_len), 1) < len_ref[i]
        scores = jnp.where(live, scores, -jnp.inf)
        top = jnp.max(scores, axis=1, keepdims=True)
        e = jnp.exp(scores - top)
        w = (e / jnp.sum(e, axis=1, keepdims=True)).astype(BF16)
        context = lax.dot_general(
            w,
            cache_s[i, pl.ds(0, LATENT), :],
            (((1,), (1,)), ((), ())),
            preferred_element_type=F32,
        )
        for k in range(LATENT // 128):
            ctx_s[k, pl.ds(i, heads, stride=rows_pad), :] = context[:, k * 128 : (k + 1) * 128]
        return carry

    lax.fori_loop(0, tokens, token_step, 0, unroll=UNROLL)

    def ag_copy(c, origin, right):
        return pltpu.make_async_remote_copy(
            src_ref=hbuf.at[c, origin],
            dst_ref=hbuf.at[c, origin],
            send_sem=ag_send.at[c, origin, 0 if right else 1],
            recv_sem=ag_recv.at[c, origin],
            device_id=(g, d + 1 if right else d - 1, t),
            device_id_type=MESH,
        )

    def ag_each(c, stage, act):
        @pl.when((d >= stage) & (d < dp_count - 1))
        def _():
            act(ag_copy(c, d - stage, True), stage)

        @pl.when((d + stage < dp_count) & (d > 0))
        def _():
            act(ag_copy(c, d + stage, False), stage)

    def pass_on(copy, stage):
        if stage:
            copy.wait_recv()
        copy.start()

    def last_arrival(c):
        @pl.when(d == dp_count - 1)
        def _():
            for o in range(dp_count - 1):
                ag_copy(c, o, False).wait_recv()

        @pl.when(d == 0)
        def _():
            for o in range(1, dp_count):
                ag_copy(c, o, True).wait_recv()

    def forward(step):
        for stage in range(1, dp_count - 1):
            c = step - stage
            if 0 <= c < chunks:
                ag_each(c, stage, pass_on)

    for c in range(chunks):
        vu_copies[c].wait()
        for hl in range(hpc):
            h = c * hpc + hl
            rows = jnp.concatenate(
                [ctx_s[k, pl.ds(h * rows_pad, rows_pad), :] for k in range(LATENT // 128)], axis=1
            ).astype(BF16)
            out = jnp.dot(rows, vu_s[h], preferred_element_type=F32)
            pack_s[pl.ds(hl * tokens, tokens), :] = out[:tokens]
        hbuf[c, d] = pack_s[...].astype(BF16)
        if c == 0:
            pl.semaphore_wait(barrier, peers - 1)
        ag_each(c, 0, pass_on)
        forward(c)

    n_tile = 256
    n_count = wo_s.shape[1] // n_tile
    for c in range(chunks):
        forward(chunks + c)
        wo_copies[c].wait()
        last_arrival(c)
        for src in range(dp_count):
            block = hbuf[c, src].astype(F32)
            for hl in range(hpc):
                lhs_s[pl.ds(src * tokens, tokens), pl.ds(hl * VHEAD, VHEAD)] = block[
                    hl * tokens : (hl + 1) * tokens
                ]
        left = lhs_s[...].astype(BF16)
        for n in range(n_count):
            sl = pl.ds(n * n_tile, n_tile)
            out = jnp.dot(left, wo_s[pl.ds(c * kc, kc), sl], preferred_element_type=F32)
            stg[:, sl] = out if c == 0 else stg[:, sl] + out

    for j in range(tp_count):
        piece = jnp.where(lane < cols, stg[:, pl.ds(j * cols, pad)], 0.0)
        red_send[j] = piece.astype(BF16)
        own_s[j] = own_s[j] + piece

    def rs_copy(o):
        peer = lax.rem(t + o, tp_count)
        return pltpu.make_async_remote_copy(
            src_ref=red_send.at[peer],
            dst_ref=red_recv.at[t],
            send_sem=rs_send.at[o],
            recv_sem=rs_recv.at[t],
            device_id=(g, d, peer),
            device_id_type=MESH,
        )

    def rs_arrival(o):
        src = lax.rem(t + o, tp_count)
        return pltpu.make_async_remote_copy(
            src_ref=red_send.at[src],
            dst_ref=red_recv.at[src],
            send_sem=rs_send.at[o],
            recv_sem=rs_recv.at[src],
            device_id=(g, d, src),
            device_id_type=MESH,
        )

    for o in range(1, tp_count):
        rs_copy(o).start()
    total = own_s[t]
    for o in range(1, tp_count):
        rs_arrival(o).wait_recv()
        total = total + red_recv[lax.rem(t + o, tp_count)].astype(F32)
    stream = total.astype(BF16)
    attn_ref[...] = stream[:, :cols]

    packed = jnp.zeros((16 * dp_count, 128), F32)
    for q in range(4):
        packed = packed + jnp.dot(
            onehot_s[q], stream[:, q * 128 : (q + 1) * 128], preferred_element_type=F32
        )
    packed = packed.astype(BF16)
    for p in range(dp_count):
        disp[p] = packed[p * 16 : (p + 1) * 16]

    def dx_copy(o):
        other = lax.rem(me + o, peers)
        return pltpu.make_async_remote_copy(
            src_ref=disp.at[other // tp_count],
            dst_ref=xrecv.at[me],
            send_sem=dx_send.at[o],
            recv_sem=dx_recv.at[me],
            device_id=(g, other // tp_count, lax.rem(other, tp_count)),
            device_id_type=MESH,
        )

    def dx_arrival(o):
        src = lax.rem(me + o, peers)
        return pltpu.make_async_remote_copy(
            src_ref=disp.at[0],
            dst_ref=xrecv.at[src],
            send_sem=dx_send.at[o],
            recv_sem=dx_recv.at[src],
            device_id=(g, src // tp_count, lax.rem(src, tp_count)),
            device_id_type=MESH,
        )

    for o in range(1, peers):
        dx_copy(o).start()
    xrecv[me] = disp[d]
    wg_copy.wait()
    wu_copy.wait()

    acc_g = jnp.zeros((16, ff), F32)
    acc_u = jnp.zeros((16, ff), F32)
    squares = jnp.zeros((16, 128), F32)

    def expert_piece(src, carry):
        acc_g, acc_u, squares = carry
        values = xrecv[src].astype(F32)
        scaled = values * gain_s[src]
        left = jnp.concatenate(
            [jnp.where(group == q, scaled, 0.0) for q in range(4)], axis=1
        ).astype(BF16)
        sl = pl.ds(pl.multiple_of(src * cols, 64), pad)
        acc_g = acc_g + jnp.dot(left, wg_s[sl, :], preferred_element_type=F32)
        acc_u = acc_u + jnp.dot(left, wu_s[sl, :], preferred_element_type=F32)
        return acc_g, acc_u, squares + values * values

    carry = expert_piece(me, (acc_g, acc_u, squares))

    def expert_step(o, carry):
        dx_arrival(o).wait_recv()
        return expert_piece(lax.rem(me + o, peers), carry)

    acc_g, acc_u, squares = lax.fori_loop(1, peers, expert_step, carry)

    def fold(a):
        return a[0:4] + a[4:8] + a[8:12] + a[12:16]

    mean_square = fold(jnp.sum(squares, axis=1, keepdims=True)) / model
    scale = lax.rsqrt(mean_square + 1e-06)
    gate_proj = fold(acc_g) * scale
    up_proj = fold(acc_u) * scale
    hidden = sg_s[0:4, 0:1] * (gate_proj / (1.0 + jnp.exp(-gate_proj))) * up_proj
    hid_ref[0] = hidden[0:capacity].astype(BF16)

    for c in range(chunks):
        for stage in range(dp_count - 1):
            ag_each(c, stage, lambda copy, stage: copy.wait_send())
    for o in range(1, tp_count):
        rs_copy(o).wait_send()
    for o in range(1, peers):
        dx_copy(o).wait_send()


UNROLL = 4


def fused_layer(
    queries,
    latent_cache,
    lengths,
    value_up,
    out_proj,
    residual,
    expert_ids,
    gate_weights,
    placement,
    norm_gain,
    w_gate,
    w_up,
):
    dp_count = lax.axis_size("dp")
    tp_count = lax.axis_size("tensor")
    all_tokens = expert_ids.shape[0]
    capacity = max(2, all_tokens * TOPK * 2 // EXPERTS)
    tokens, heads, width = queries.shape
    cols = residual.shape[1] // tp_count
    model = norm_gain.shape[0]
    ff = w_gate.shape[2]
    pad = 512
    chunks = 4
    rows_pad = 16
    peers = dp_count * tp_count
    hpc = heads // chunks
    hbm = pl.BlockSpec(memory_space=pl.ANY)
    vmem = pl.BlockSpec(memory_space=pltpu.VMEM)
    smem = pl.BlockSpec(memory_space=pltpu.SMEM)
    dma = pltpu.SemaphoreType.DMA
    return pl.pallas_call(
        functools.partial(layer_kernel, dp_count, tp_count),
        out_shape=(
            jax.ShapeDtypeStruct((all_tokens, cols), BF16),
            jax.ShapeDtypeStruct((1, capacity, ff), BF16),
        ),
        in_specs=[hbm, hbm, smem, hbm, hbm, vmem, vmem, vmem, vmem, vmem, hbm, hbm],
        out_specs=(vmem, vmem),
        scratch_shapes=[
            pltpu.VMEM((tokens, heads, width), BF16),
            pltpu.VMEM((tokens, width, latent_cache.shape[1]), BF16),
            pltpu.VMEM(value_up.shape, BF16),
            pltpu.VMEM(out_proj.shape, BF16),
            pltpu.VMEM((model + pad - cols, ff), BF16),
            pltpu.VMEM((model + pad - cols, ff), BF16),
            pltpu.VMEM((LATENT // 128, heads * rows_pad, 128), F32),
            pltpu.VMEM((chunks, dp_count, hpc * tokens, VHEAD), BF16),
            pltpu.VMEM((hpc * tokens, VHEAD), F32),
            pltpu.VMEM((dp_count * tokens, hpc * VHEAD), F32),
            pltpu.VMEM((model // 128 + 8, 128), F32),
            pltpu.VMEM((peers, 16, 128), F32),
            pltpu.VMEM((all_tokens, tp_count * cols + 128), F32),
            pltpu.VMEM((tp_count, all_tokens, pad), F32),
            pltpu.VMEM((tp_count, all_tokens, pad), BF16),
            pltpu.VMEM((tp_count, all_tokens, pad), BF16),
            pltpu.VMEM((4, 16 * dp_count, all_tokens), BF16),
            pltpu.VMEM((dp_count, 16, 128), BF16),
            pltpu.VMEM((peers, 16, 128), BF16),
            pltpu.VMEM((8, 128), F32),
            dma((2,)),
            dma((chunks,)),
            dma((chunks,)),
            dma((2,)),
            dma((chunks, dp_count, 2)),
            dma((chunks, dp_count)),
            dma((tp_count,)),
            dma((tp_count,)),
            dma((peers,)),
            dma((peers,)),
        ],
        compiler_params=pltpu.CompilerParams(
            collective_id=0, has_side_effects=True, vmem_limit_bytes=58 * 1024 * 1024
        ),
    )(
        queries,
        jnp.swapaxes(latent_cache, 1, 2),
        lengths,
        value_up,
        out_proj,
        residual,
        expert_ids.T,
        gate_weights.T,
        placement.reshape(1, -1),
        norm_gain.reshape(-1, 128),
        w_gate,
        w_up,
    )


def slot_table(expert_ids, placement, held_count, capacity):
    flat_ids = expert_ids.reshape(-1)
    id_match = flat_ids[:, None] == jnp.arange(EXPERTS, dtype=jnp.int32)[None, :]
    position = jnp.sum(jnp.where(id_match, placement[None, :], 0), axis=1)
    chosen = (position[:, None] == jnp.arange(held_count, dtype=jnp.int32)[None, :]).astype(
        jnp.int32
    )
    earlier = jnp.cumsum(chosen, axis=0) - chosen
    slot_index = jnp.sum(chosen * earlier, axis=1)
    kept_slot = (position < held_count) & (slot_index < capacity)
    target = jnp.where(kept_slot, position * capacity + slot_index, held_count * capacity)
    return target.reshape(expert_ids.shape)


def on_device(
    queries,
    latent_cache,
    lengths,
    value_up,
    out_proj,
    residual,
    expert_ids,
    gate_weights,
    placement,
    norm_gain,
    w_gate,
    w_up,
):
    dp_count = lax.axis_size("dp")
    tensor_count = lax.axis_size("tensor")
    token_count = expert_ids.shape[0]
    local_experts = w_gate.shape[0]
    held_count = local_experts * dp_count
    capacity = max(2, token_count * TOPK * 2 // EXPERTS)
    score_scale = (VHEAD + ROPE) ** (-0.5)
    scores = (
        jnp.einsum("thc,tsc->ths", queries, latent_cache, preferred_element_type=jnp.float32)
        * score_scale
    )
    live_keys = (
        jnp.arange(latent_cache.shape[1], dtype=jnp.int32)[None, None, :] < lengths[:, None, None]
    )
    scores = jnp.where(live_keys, scores, -jnp.inf)
    row_max = jnp.max(scores, axis=2, keepdims=True)
    exponent = jnp.exp(scores - row_max)
    attention_weights = (exponent / jnp.sum(exponent, axis=2, keepdims=True)).astype(jnp.bfloat16)
    context = jnp.einsum(
        "ths,tsc->thc",
        attention_weights,
        latent_cache[:, :, :LATENT],
        preferred_element_type=jnp.float32,
    ).astype(jnp.bfloat16)
    head_out = jnp.einsum(
        "thc,hcv->thv", context, value_up, preferred_element_type=jnp.float32
    ).astype(jnp.bfloat16)
    head_out = head_out.reshape(head_out.shape[0], -1)
    partial_sum = jnp.dot(
        lax.all_gather(head_out, "dp", axis=0, tiled=True),
        out_proj,
        preferred_element_type=jnp.float32,
    )
    target = slot_table(expert_ids, placement, held_count, capacity)
    slot_ids = jnp.arange(held_count * capacity, dtype=jnp.int32)
    slot_match = target[:, :, None] == slot_ids[None, None, :]
    onehot = jnp.any(slot_match, axis=1).astype(jnp.bfloat16)
    gate_all = jnp.sum(jnp.where(slot_match, gate_weights[:, :, None], 0.0), axis=(0, 1))
    owner_span = local_experts * capacity
    owner_index = lax.axis_index("dp")
    slot_gate = lax.dynamic_slice_in_dim(gate_all, owner_index * owner_span, owner_span).reshape(
        local_experts, capacity
    )
    gain_values = norm_gain.astype(jnp.float32)
    tensor_pos = lax.axis_index("tensor")
    summed_all = lax.psum(partial_sum, "tensor")
    stream_cols = (summed_all + residual.astype(jnp.float32)).astype(jnp.bfloat16)
    col_width = stream_cols.shape[1] // tensor_count
    attn_out = lax.dynamic_slice_in_dim(stream_cols, tensor_pos * col_width, col_width, 1)
    buffer = jnp.einsum(
        "td,tc->dc", onehot, stream_cols, preferred_element_type=jnp.float32
    ).astype(jnp.bfloat16)
    buffer = buffer.reshape(held_count, capacity, -1)
    values = lax.all_to_all(buffer, "dp", split_axis=0, concat_axis=2, tiled=True).astype(
        jnp.float32
    )
    mean_square = jnp.mean(values * values, axis=-1, keepdims=True)
    normed = (values * lax.rsqrt(mean_square + 1e-06) * gain_values).astype(jnp.bfloat16)
    gate_proj = jnp.einsum("end,edf->enf", normed, w_gate, preferred_element_type=jnp.float32)
    up_proj = jnp.einsum("end,edf->enf", normed, w_up, preferred_element_type=jnp.float32)
    hidden = jax.nn.silu(gate_proj) * up_proj
    result = (slot_gate[:, :, None] * hidden).astype(jnp.bfloat16)
    return (attn_out, result)


def solution(mesh):
    in_specs = (
        P(("groups", "dp"), "tensor", None),
        P(("groups", "dp"), None, None),
        P(("groups", "dp")),
        P("tensor", None, None),
        P("tensor", "dp"),
        P("groups", "dp"),
        P("groups", None),
        P("groups", None),
        P("groups"),
        P(),
        P("dp", None, "tensor"),
        P("dp", None, "tensor"),
    )
    out_specs = (P("groups", ("dp", "tensor")), P(("groups", "dp"), None, "tensor"))

    def layer(*args):
        token_count = args[6].shape[0]
        capacity = max(2, token_count * TOPK * 2 // EXPERTS)
        cols = args[5].shape[1] // mesh.shape["tensor"]
        fits = (
            args[10].shape[0] == 1
            and capacity <= 4
            and 384 < cols <= 512
            and cols % 64 == 0
            and args[5].shape[1] % 256 == 0
            and args[0].shape[0] <= 16
            and args[0].shape[1] % 4 == 0
            and mesh.shape["dp"] < 8
            and token_count % 16 == 0
            and args[0].shape[1] // 4 * args[0].shape[0] % 16 == 0
        )
        return (fused_layer if fits else on_device)(*args)

    return jax.shard_map(
        layer, mesh=mesh, in_specs=in_specs, out_specs=out_specs, check_vma=False
    )
```

```python
import functools

import jax
import jax.numpy as jnp
from jax import lax
from jax.experimental import pallas as pl
from jax.experimental.pallas import tpu as pltpu
from jax.sharding import PartitionSpec as P

LATENT = 512
ROPE = 64
VHEAD = 128
EXPERTS = 256
TOPK = 8
F32 = jnp.float32
BF16 = jnp.bfloat16
MESH = pl.DeviceIdType.MESH


def layer_kernel(
    dp_count,
    tp_count,
    q_hbm,
    cache_hbm,
    len_ref,
    vu_hbm,
    wo_hbm,
    res_ref,
    ids_ref,
    gates_ref,
    place_ref,
    gain_ref,
    wg_hbm,
    wu_hbm,
    attn_ref,
    hid_ref,
    q_s,
    cache_s,
    vu_s,
    wo_s,
    wg_s,
    wu_s,
    ctx_s,
    hbuf,
    pack_s,
    lhs_s,
    gain_a,
    gain_s,
    stg,
    own_s,
    red_send,
    red_recv,
    onehot_s,
    disp,
    xrecv,
    sg_s,
    in_sem,
    vu_sem,
    wo_sem,
    we_sem,
    ag_send,
    ag_recv,
    rs_send,
    rs_recv,
    dx_send,
    dx_recv,
):
    g = lax.axis_index("groups")
    d = lax.axis_index("dp")
    t = lax.axis_index("tensor")
    peers = dp_count * tp_count
    me = d * tp_count + t
    tokens, heads, width = q_s.shape
    rows_pad = ctx_s.shape[1] // heads
    chunks = hbuf.shape[0]
    hpc = heads // chunks
    kc = hpc * VHEAD
    cols = attn_ref.shape[1]
    pad = own_s.shape[2]
    all_tokens = attn_ref.shape[0]
    model = wg_hbm.shape[1]
    ff = wg_hbm.shape[2]
    capacity = hid_ref.shape[1]

    q_copy = pltpu.make_async_copy(q_hbm, q_s, in_sem.at[0])
    c_copy = pltpu.make_async_copy(cache_hbm, cache_s, in_sem.at[1])
    q_copy.start()
    c_copy.start()

    barrier = pltpu.get_barrier_semaphore()
    for o in range(1, peers):
        other = lax.rem(me + o, peers)
        pl.semaphore_signal(
            barrier,
            inc=1,
            device_id=(g, other // tp_count, lax.rem(other, tp_count)),
            device_id_type=MESH,
        )

    vu_copies = [
        pltpu.make_async_copy(
            vu_hbm.at[pl.ds(c * hpc, hpc)], vu_s.at[pl.ds(c * hpc, hpc)], vu_sem.at[c]
        )
        for c in range(chunks)
    ]
    wo_copies = [
        pltpu.make_async_copy(
            wo_hbm.at[pl.ds(c * kc, kc)], wo_s.at[pl.ds(c * kc, kc)], wo_sem.at[c]
        )
        for c in range(chunks)
    ]
    wg_copy = pltpu.make_async_copy(wg_hbm.at[0], wg_s.at[pl.ds(0, model)], we_sem.at[0])
    wu_copy = pltpu.make_async_copy(wu_hbm.at[0], wu_s.at[pl.ds(0, model)], we_sem.at[1])
    ids = ids_ref[...]
    gates = gates_ref[...]
    place = place_ref[...]
    expert_iota = lax.broadcasted_iota(jnp.int32, place.shape, 1)

    def choice(position):
        expert = jnp.sum(jnp.where(place == position, expert_iota, 0), axis=1, keepdims=True)
        return ids == expert

    row8 = lax.broadcasted_iota(jnp.int32, (8, all_tokens), 0)
    match = jnp.zeros((8, all_tokens), F32)
    for p in range(dp_count):
        hit = jnp.sum(choice(p).astype(F32), axis=0, keepdims=True)
        match = jnp.where(row8 == p, hit, match)
    own_choice = choice(d)
    own_hit = jnp.sum(own_choice.astype(F32), axis=0, keepdims=True)
    own_gate = jnp.sum(jnp.where(own_choice, gates, 0.0), axis=0, keepdims=True)
    match = jnp.where(row8 == dp_count, own_hit, match)
    up_r = lax.broadcasted_iota(jnp.int32, (all_tokens, all_tokens), 0)
    up_c = lax.broadcasted_iota(jnp.int32, (all_tokens, all_tokens), 1)
    upper = jnp.where(up_r < up_c, 1.0, 0.0).astype(BF16)
    earlier = jnp.dot(match.astype(BF16), upper, preferred_element_type=F32)
    shape = (16 * dp_count, all_tokens)
    rep_m = jnp.concatenate(
        [jnp.broadcast_to(match[p : p + 1], (16, all_tokens)) for p in range(dp_count)], axis=0
    )
    rep_e = jnp.concatenate(
        [jnp.broadcast_to(earlier[p : p + 1], (16, all_tokens)) for p in range(dp_count)], axis=0
    )
    r_iota = lax.broadcasted_iota(jnp.int32, shape, 0)
    slot = r_iota & 3
    quarter = (r_iota >> 2) & 3
    kept = jnp.where((rep_e == slot.astype(F32)) & (slot < capacity), rep_m, 0.0)
    for q in range(4):
        onehot_s[q] = jnp.where(quarter == q, kept, 0.0).astype(BF16)
    own_e = jnp.broadcast_to(earlier[dp_count : dp_count + 1], (8, all_tokens))
    own_g = jnp.broadcast_to(own_gate * own_hit, (8, all_tokens))
    sg_s[...] = jnp.broadcast_to(
        jnp.sum(
            jnp.where((own_e == row8.astype(F32)) & (row8 < capacity), own_g, 0.0),
            axis=1,
            keepdims=True,
        ),
        sg_s.shape,
    )

    ctx_s[...] = jnp.zeros_like(ctx_s)
    wg_s[pl.ds(model, wg_s.shape[0] - model), :] = jnp.zeros((wg_s.shape[0] - model, ff), BF16)
    wu_s[pl.ds(model, wu_s.shape[0] - model), :] = jnp.zeros((wu_s.shape[0] - model, ff), BF16)
    total_cols = tp_count * cols
    stg[:, pl.ds(total_cols, stg.shape[1] - total_cols)] = jnp.zeros(
        (all_tokens, stg.shape[1] - total_cols), F32
    )
    stg[:, pl.ds(0, total_cols)] = res_ref[...].astype(F32)
    lane = lax.broadcasted_iota(jnp.int32, (all_tokens, pad), 1)
    for j in range(tp_count):
        own_s[j] = jnp.where(lane < cols, stg[:, pl.ds(j * cols, pad)], 0.0)

    gain_rows = gain_ref.shape[0]
    gain_a[pl.ds(0, gain_rows), :] = gain_ref[...].astype(F32)
    gain_a[pl.ds(gain_rows, 8), :] = jnp.zeros((8, 128), F32)
    half = lax.broadcasted_iota(jnp.int32, (1, 128), 1) >= 64
    group = lax.broadcasted_iota(jnp.int32, (16, 128), 0) >> 2
    for src in range(peers):
        first, odd = divmod(src * cols, 128)
        block = jnp.zeros((16, 128), F32)
        for q in range(4):
            row = gain_a[pl.ds(first + q, 1), :]
            if odd:
                row = pltpu.roll(jnp.where(half, row, gain_a[pl.ds(first + q + 1, 1), :]), 64, 1)
            block = jnp.where(group == q, row, block)
        gain_s[src] = block

    q_copy.wait()
    c_copy.wait()
    for cp in vu_copies:
        cp.start()
    for cp in wo_copies:
        cp.start()
    wg_copy.start()
    wu_copy.start()

    score_scale = (VHEAD + ROPE) ** (-0.5)
    ctx_len = cache_s.shape[2]

    def token_step(i, carry):
        scores = jnp.dot(q_s[i], cache_s[i], preferred_element_type=F32) * score_scale
        live = lax.broadcasted_iota(jnp.int32, (heads, ctx_len), 1) < len_ref[i]
        scores = jnp.where(live, scores, -jnp.inf)
        top = jnp.max(scores, axis=1, keepdims=True)
        e = jnp.exp(scores - top)
        w = (e / jnp.sum(e, axis=1, keepdims=True)).astype(BF16)
        context = lax.dot_general(
            w,
            cache_s[i, pl.ds(0, LATENT), :],
            (((1,), (1,)), ((), ())),
            preferred_element_type=F32,
        )
        for k in range(LATENT // 128):
            ctx_s[k, pl.ds(i, heads, stride=rows_pad), :] = context[:, k * 128 : (k + 1) * 128]
        return carry

    lax.fori_loop(0, tokens, token_step, 0, unroll=UNROLL)

    def ag_copy(c, stage, right):
        return pltpu.make_async_remote_copy(
            src_ref=hbuf.at[c, d],
            dst_ref=hbuf.at[c, d],
            send_sem=ag_send.at[c, stage, 0 if right else 1],
            recv_sem=ag_recv.at[c, d],
            device_id=(g, d + stage + 1 if right else d - stage - 1, t),
            device_id_type=MESH,
        )

    def ag_each(c, stage, act):
        @pl.when(d + stage + 1 < dp_count)
        def _():
            act(ag_copy(c, stage, True), stage)

        @pl.when(d - stage - 1 >= 0)
        def _():
            act(ag_copy(c, stage, False), stage)

    def launch(copy, stage):
        copy.start()

    def last_arrival(c):
        for o in range(1, dp_count):
            src = lax.rem(d + o, dp_count)
            pltpu.make_async_remote_copy(
                src_ref=hbuf.at[c, src],
                dst_ref=hbuf.at[c, src],
                send_sem=ag_send.at[c, 0, 0],
                recv_sem=ag_recv.at[c, src],
                device_id=(g, src, t),
                device_id_type=MESH,
            ).wait_recv()

    for c in range(chunks):
        vu_copies[c].wait()
        for hl in range(hpc):
            h = c * hpc + hl
            rows = jnp.concatenate(
                [ctx_s[k, pl.ds(h * rows_pad, rows_pad), :] for k in range(LATENT // 128)], axis=1
            ).astype(BF16)
            out = jnp.dot(rows, vu_s[h], preferred_element_type=F32)
            pack_s[pl.ds(hl * tokens, tokens), :] = out[:tokens]
        hbuf[c, d] = pack_s[...].astype(BF16)
        if c == 0:
            pl.semaphore_wait(barrier, peers - 1)
        for stage in reversed(range(dp_count - 1)):
            ag_each(c, stage, launch)

    n_tile = 256
    n_count = wo_s.shape[1] // n_tile
    for c in range(chunks):
        wo_copies[c].wait()
        last_arrival(c)
        for src in range(dp_count):
            block = hbuf[c, src].astype(F32)
            for hl in range(hpc):
                lhs_s[pl.ds(src * tokens, tokens), pl.ds(hl * VHEAD, VHEAD)] = block[
                    hl * tokens : (hl + 1) * tokens
                ]
        left = lhs_s[...].astype(BF16)
        for n in range(n_count):
            sl = pl.ds(n * n_tile, n_tile)
            out = jnp.dot(left, wo_s[pl.ds(c * kc, kc), sl], preferred_element_type=F32)
            stg[:, sl] = out if c == 0 else stg[:, sl] + out

    for j in range(tp_count):
        piece = jnp.where(lane < cols, stg[:, pl.ds(j * cols, pad)], 0.0)
        red_send[j] = piece.astype(BF16)
        own_s[j] = own_s[j] + piece

    def rs_copy(o):
        peer = lax.rem(t + o, tp_count)
        return pltpu.make_async_remote_copy(
            src_ref=red_send.at[peer],
            dst_ref=red_recv.at[t],
            send_sem=rs_send.at[o],
            recv_sem=rs_recv.at[t],
            device_id=(g, d, peer),
            device_id_type=MESH,
        )

    def rs_arrival(o):
        src = lax.rem(t + o, tp_count)
        return pltpu.make_async_remote_copy(
            src_ref=red_send.at[src],
            dst_ref=red_recv.at[src],
            send_sem=rs_send.at[o],
            recv_sem=rs_recv.at[src],
            device_id=(g, d, src),
            device_id_type=MESH,
        )

    for o in range(1, tp_count):
        rs_copy(o).start()
    total = own_s[t]
    for o in range(1, tp_count):
        rs_arrival(o).wait_recv()
        total = total + red_recv[lax.rem(t + o, tp_count)].astype(F32)
    stream = total.astype(BF16)
    attn_ref[...] = stream[:, :cols]

    packed = jnp.zeros((16 * dp_count, 128), F32)
    for q in range(4):
        packed = packed + jnp.dot(
            onehot_s[q], stream[:, q * 128 : (q + 1) * 128], preferred_element_type=F32
        )
    packed = packed.astype(BF16)
    for p in range(dp_count):
        disp[p] = packed[p * 16 : (p + 1) * 16]

    def dx_copy(o):
        other = lax.rem(me + o, peers)
        return pltpu.make_async_remote_copy(
            src_ref=disp.at[other // tp_count],
            dst_ref=xrecv.at[me],
            send_sem=dx_send.at[o],
            recv_sem=dx_recv.at[me],
            device_id=(g, other // tp_count, lax.rem(other, tp_count)),
            device_id_type=MESH,
        )

    def dx_arrival(o):
        src = lax.rem(me + o, peers)
        return pltpu.make_async_remote_copy(
            src_ref=disp.at[0],
            dst_ref=xrecv.at[src],
            send_sem=dx_send.at[o],
            recv_sem=dx_recv.at[src],
            device_id=(g, src // tp_count, lax.rem(src, tp_count)),
            device_id_type=MESH,
        )

    for o in range(1, peers):
        dx_copy(o).start()
    xrecv[me] = disp[d]
    wg_copy.wait()
    wu_copy.wait()

    acc_g = jnp.zeros((16, ff), F32)
    acc_u = jnp.zeros((16, ff), F32)
    squares = jnp.zeros((16, 128), F32)

    def expert_piece(src, carry):
        acc_g, acc_u, squares = carry
        values = xrecv[src].astype(F32)
        scaled = values * gain_s[src]
        left = jnp.concatenate(
            [jnp.where(group == q, scaled, 0.0) for q in range(4)], axis=1
        ).astype(BF16)
        sl = pl.ds(pl.multiple_of(src * cols, 64), pad)
        acc_g = acc_g + jnp.dot(left, wg_s[sl, :], preferred_element_type=F32)
        acc_u = acc_u + jnp.dot(left, wu_s[sl, :], preferred_element_type=F32)
        return acc_g, acc_u, squares + values * values

    carry = expert_piece(me, (acc_g, acc_u, squares))

    def expert_step(o, carry):
        dx_arrival(o).wait_recv()
        return expert_piece(lax.rem(me + o, peers), carry)

    acc_g, acc_u, squares = lax.fori_loop(1, peers, expert_step, carry, unroll=True)

    def fold(a):
        return a[0:4] + a[4:8] + a[8:12] + a[12:16]

    mean_square = fold(jnp.sum(squares, axis=1, keepdims=True)) / model
    scale = lax.rsqrt(mean_square + 1e-06)
    gate_proj = fold(acc_g) * scale
    up_proj = fold(acc_u) * scale
    hidden = sg_s[0:4, 0:1] * (gate_proj / (1.0 + jnp.exp(-gate_proj))) * up_proj
    hid_ref[0] = hidden[0:capacity].astype(BF16)

    for c in range(chunks):
        for stage in range(dp_count - 1):
            ag_each(c, stage, lambda copy, stage: copy.wait_send())
    for o in range(1, tp_count):
        rs_copy(o).wait_send()
    for o in range(1, peers):
        dx_copy(o).wait_send()


UNROLL = 4


def fused_layer(
    queries,
    latent_cache,
    lengths,
    value_up,
    out_proj,
    residual,
    expert_ids,
    gate_weights,
    placement,
    norm_gain,
    w_gate,
    w_up,
):
    dp_count = lax.axis_size("dp")
    tp_count = lax.axis_size("tensor")
    all_tokens = expert_ids.shape[0]
    capacity = max(2, all_tokens * TOPK * 2 // EXPERTS)
    tokens, heads, width = queries.shape
    cols = residual.shape[1] // tp_count
    model = norm_gain.shape[0]
    ff = w_gate.shape[2]
    pad = 512
    chunks = 4
    rows_pad = 16
    peers = dp_count * tp_count
    hpc = heads // chunks
    hbm = pl.BlockSpec(memory_space=pl.ANY)
    vmem = pl.BlockSpec(memory_space=pltpu.VMEM)
    smem = pl.BlockSpec(memory_space=pltpu.SMEM)
    dma = pltpu.SemaphoreType.DMA
    return pl.pallas_call(
        functools.partial(layer_kernel, dp_count, tp_count),
        out_shape=(
            pltpu.VMEM((all_tokens, cols), BF16),
            pltpu.VMEM((1, capacity, ff), BF16),
        ),
        in_specs=[hbm, hbm, smem, hbm, hbm, vmem, vmem, vmem, vmem, vmem, hbm, hbm],
        out_specs=(vmem, vmem),
        scratch_shapes=[
            pltpu.VMEM((tokens, heads, width), BF16),
            pltpu.VMEM((tokens, width, latent_cache.shape[1]), BF16),
            pltpu.VMEM(value_up.shape, BF16),
            pltpu.VMEM(out_proj.shape, BF16),
            pltpu.VMEM((model + pad - cols, ff), BF16),
            pltpu.VMEM((model + pad - cols, ff), BF16),
            pltpu.VMEM((LATENT // 128, heads * rows_pad, 128), F32),
            pltpu.VMEM((chunks, dp_count, hpc * tokens, VHEAD), BF16),
            pltpu.VMEM((hpc * tokens, VHEAD), F32),
            pltpu.VMEM((dp_count * tokens, hpc * VHEAD), F32),
            pltpu.VMEM((model // 128 + 8, 128), F32),
            pltpu.VMEM((peers, 16, 128), F32),
            pltpu.VMEM((all_tokens, tp_count * cols + 128), F32),
            pltpu.VMEM((tp_count, all_tokens, pad), F32),
            pltpu.VMEM((tp_count, all_tokens, pad), BF16),
            pltpu.VMEM((tp_count, all_tokens, pad), BF16),
            pltpu.VMEM((4, 16 * dp_count, all_tokens), BF16),
            pltpu.VMEM((dp_count, 16, 128), BF16),
            pltpu.VMEM((peers, 16, 128), BF16),
            pltpu.VMEM((8, 128), F32),
            dma((2,)),
            dma((chunks,)),
            dma((chunks,)),
            dma((2,)),
            dma((chunks, dp_count, 2)),
            dma((chunks, dp_count)),
            dma((tp_count,)),
            dma((tp_count,)),
            dma((peers,)),
            dma((peers,)),
        ],
        compiler_params=pltpu.CompilerParams(
            collective_id=0, has_side_effects=True, vmem_limit_bytes=58 * 1024 * 1024
        ),
    )(
        queries,
        jnp.swapaxes(latent_cache, 1, 2),
        lengths,
        value_up,
        out_proj,
        residual,
        expert_ids.T,
        gate_weights.T,
        placement.reshape(1, -1),
        norm_gain.reshape(-1, 128),
        w_gate,
        w_up,
    )


def slot_table(expert_ids, placement, held_count, capacity):
    flat_ids = expert_ids.reshape(-1)
    id_match = flat_ids[:, None] == jnp.arange(EXPERTS, dtype=jnp.int32)[None, :]
    position = jnp.sum(jnp.where(id_match, placement[None, :], 0), axis=1)
    chosen = (position[:, None] == jnp.arange(held_count, dtype=jnp.int32)[None, :]).astype(
        jnp.int32
    )
    earlier = jnp.cumsum(chosen, axis=0) - chosen
    slot_index = jnp.sum(chosen * earlier, axis=1)
    kept_slot = (position < held_count) & (slot_index < capacity)
    target = jnp.where(kept_slot, position * capacity + slot_index, held_count * capacity)
    return target.reshape(expert_ids.shape)


def on_device(
    queries,
    latent_cache,
    lengths,
    value_up,
    out_proj,
    residual,
    expert_ids,
    gate_weights,
    placement,
    norm_gain,
    w_gate,
    w_up,
):
    dp_count = lax.axis_size("dp")
    tensor_count = lax.axis_size("tensor")
    token_count = expert_ids.shape[0]
    local_experts = w_gate.shape[0]
    held_count = local_experts * dp_count
    capacity = max(2, token_count * TOPK * 2 // EXPERTS)
    score_scale = (VHEAD + ROPE) ** (-0.5)
    scores = (
        jnp.einsum("thc,tsc->ths", queries, latent_cache, preferred_element_type=jnp.float32)
        * score_scale
    )
    live_keys = (
        jnp.arange(latent_cache.shape[1], dtype=jnp.int32)[None, None, :] < lengths[:, None, None]
    )
    scores = jnp.where(live_keys, scores, -jnp.inf)
    row_max = jnp.max(scores, axis=2, keepdims=True)
    exponent = jnp.exp(scores - row_max)
    attention_weights = (exponent / jnp.sum(exponent, axis=2, keepdims=True)).astype(jnp.bfloat16)
    context = jnp.einsum(
        "ths,tsc->thc",
        attention_weights,
        latent_cache[:, :, :LATENT],
        preferred_element_type=jnp.float32,
    ).astype(jnp.bfloat16)
    head_out = jnp.einsum(
        "thc,hcv->thv", context, value_up, preferred_element_type=jnp.float32
    ).astype(jnp.bfloat16)
    head_out = head_out.reshape(head_out.shape[0], -1)
    partial_sum = jnp.dot(
        lax.all_gather(head_out, "dp", axis=0, tiled=True),
        out_proj,
        preferred_element_type=jnp.float32,
    )
    target = slot_table(expert_ids, placement, held_count, capacity)
    slot_ids = jnp.arange(held_count * capacity, dtype=jnp.int32)
    slot_match = target[:, :, None] == slot_ids[None, None, :]
    onehot = jnp.any(slot_match, axis=1).astype(jnp.bfloat16)
    gate_all = jnp.sum(jnp.where(slot_match, gate_weights[:, :, None], 0.0), axis=(0, 1))
    owner_span = local_experts * capacity
    owner_index = lax.axis_index("dp")
    slot_gate = lax.dynamic_slice_in_dim(gate_all, owner_index * owner_span, owner_span).reshape(
        local_experts, capacity
    )
    gain_values = norm_gain.astype(jnp.float32)
    tensor_pos = lax.axis_index("tensor")
    summed_all = lax.psum(partial_sum, "tensor")
    stream_cols = (summed_all + residual.astype(jnp.float32)).astype(jnp.bfloat16)
    col_width = stream_cols.shape[1] // tensor_count
    attn_out = lax.dynamic_slice_in_dim(stream_cols, tensor_pos * col_width, col_width, 1)
    buffer = jnp.einsum(
        "td,tc->dc", onehot, stream_cols, preferred_element_type=jnp.float32
    ).astype(jnp.bfloat16)
    buffer = buffer.reshape(held_count, capacity, -1)
    values = lax.all_to_all(buffer, "dp", split_axis=0, concat_axis=2, tiled=True).astype(
        jnp.float32
    )
    mean_square = jnp.mean(values * values, axis=-1, keepdims=True)
    normed = (values * lax.rsqrt(mean_square + 1e-06) * gain_values).astype(jnp.bfloat16)
    gate_proj = jnp.einsum("end,edf->enf", normed, w_gate, preferred_element_type=jnp.float32)
    up_proj = jnp.einsum("end,edf->enf", normed, w_up, preferred_element_type=jnp.float32)
    hidden = jax.nn.silu(gate_proj) * up_proj
    result = (slot_gate[:, :, None] * hidden).astype(jnp.bfloat16)
    return (attn_out, result)


def solution(mesh):
    in_specs = (
        P(("groups", "dp"), "tensor", None),
        P(("groups", "dp"), None, None),
        P(("groups", "dp")),
        P("tensor", None, None),
        P("tensor", "dp"),
        P("groups", "dp"),
        P("groups", None),
        P("groups", None),
        P("groups"),
        P(),
        P("dp", None, "tensor"),
        P("dp", None, "tensor"),
    )
    out_specs = (P("groups", ("dp", "tensor")), P(("groups", "dp"), None, "tensor"))

    def layer(*args):
        token_count = args[6].shape[0]
        capacity = max(2, token_count * TOPK * 2 // EXPERTS)
        cols = args[5].shape[1] // mesh.shape["tensor"]
        fits = (
            args[10].shape[0] == 1
            and capacity <= 4
            and 384 < cols <= 512
            and cols % 64 == 0
            and args[5].shape[1] % 256 == 0
            and args[0].shape[0] <= 16
            and args[0].shape[1] % 4 == 0
            and mesh.shape["dp"] < 8
            and token_count % 16 == 0
            and args[0].shape[1] // 4 * args[0].shape[0] % 16 == 0
        )
        return (fused_layer if fits else on_device)(*args)

    return jax.shard_map(
        layer, mesh=mesh, in_specs=in_specs, out_specs=out_specs, check_vma=False
    )
```

```python
import functools

import jax
import jax.numpy as jnp
from jax import lax
from jax.experimental import pallas as pl
from jax.experimental.pallas import tpu as pltpu
from jax.sharding import PartitionSpec as P

LATENT = 512
ROPE = 64
VHEAD = 128
EXPERTS = 256
TOPK = 8
F32 = jnp.float32
BF16 = jnp.bfloat16
MESH = pl.DeviceIdType.MESH


def layer_kernel(
    dp_count,
    tp_count,
    q_hbm,
    cache_hbm,
    len_ref,
    vu_hbm,
    wo_hbm,
    res_ref,
    ids_ref,
    gates_ref,
    place_ref,
    gain_ref,
    wg_hbm,
    wu_hbm,
    attn_ref,
    hid_ref,
    q_s,
    cache_s,
    vu_s,
    wo_s,
    wg_s,
    wu_s,
    ctx_s,
    hbuf,
    pack_s,
    lhs_s,
    gain_a,
    gain_s,
    stg,
    own_s,
    red_send,
    red_recv,
    onehot_s,
    disp,
    xrecv,
    sg_s,
    in_sem,
    vu_sem,
    wo_sem,
    we_sem,
    ag_send,
    ag_recv,
    rs_send,
    rs_recv,
    dx_send,
    dx_recv,
):
    g = lax.axis_index("groups")
    d = lax.axis_index("dp")
    t = lax.axis_index("tensor")
    peers = dp_count * tp_count
    me = d * tp_count + t
    tokens, heads, width = q_s.shape
    rows_pad = ctx_s.shape[1] // heads
    chunks = hbuf.shape[0]
    hpc = heads // chunks
    kc = hpc * VHEAD
    cols = attn_ref.shape[1]
    pad = own_s.shape[2]
    all_tokens = attn_ref.shape[0]
    model = wg_hbm.shape[1]
    ff = wg_hbm.shape[2]
    capacity = hid_ref.shape[1]

    q_copy = pltpu.make_async_copy(q_hbm, q_s, in_sem.at[0])
    c_copy = pltpu.make_async_copy(cache_hbm, cache_s, in_sem.at[1])
    q_copy.start()
    c_copy.start()

    barrier = pltpu.get_barrier_semaphore()
    for o in range(1, peers):
        other = lax.rem(me + o, peers)
        pl.semaphore_signal(
            barrier,
            inc=1,
            device_id=(g, other // tp_count, lax.rem(other, tp_count)),
            device_id_type=MESH,
        )

    vu_copies = [
        pltpu.make_async_copy(
            vu_hbm.at[pl.ds(c * hpc, hpc)], vu_s.at[pl.ds(c * hpc, hpc)], vu_sem.at[c]
        )
        for c in range(chunks)
    ]
    wo_copies = [
        pltpu.make_async_copy(
            wo_hbm.at[pl.ds(c * kc, kc)], wo_s.at[pl.ds(c * kc, kc)], wo_sem.at[c]
        )
        for c in range(chunks)
    ]
    wg_copy = pltpu.make_async_copy(wg_hbm.at[0], wg_s.at[pl.ds(0, model)], we_sem.at[0])
    wu_copy = pltpu.make_async_copy(wu_hbm.at[0], wu_s.at[pl.ds(0, model)], we_sem.at[1])
    ids = ids_ref[...]
    gates = gates_ref[...]
    place = place_ref[...]
    expert_iota = lax.broadcasted_iota(jnp.int32, place.shape, 1)

    def choice(position):
        expert = jnp.sum(jnp.where(place == position, expert_iota, 0), axis=1, keepdims=True)
        return ids == expert

    row8 = lax.broadcasted_iota(jnp.int32, (8, all_tokens), 0)
    match = jnp.zeros((8, all_tokens), F32)
    for p in range(dp_count):
        hit = jnp.sum(choice(p).astype(F32), axis=0, keepdims=True)
        match = jnp.where(row8 == p, hit, match)
    own_choice = choice(d)
    own_hit = jnp.sum(own_choice.astype(F32), axis=0, keepdims=True)
    own_gate = jnp.sum(jnp.where(own_choice, gates, 0.0), axis=0, keepdims=True)
    match = jnp.where(row8 == dp_count, own_hit, match)
    up_r = lax.broadcasted_iota(jnp.int32, (all_tokens, all_tokens), 0)
    up_c = lax.broadcasted_iota(jnp.int32, (all_tokens, all_tokens), 1)
    upper = jnp.where(up_r < up_c, 1.0, 0.0).astype(BF16)
    earlier = jnp.dot(match.astype(BF16), upper, preferred_element_type=F32)
    shape = (16 * dp_count, all_tokens)
    rep_m = jnp.concatenate(
        [jnp.broadcast_to(match[p : p + 1], (16, all_tokens)) for p in range(dp_count)], axis=0
    )
    rep_e = jnp.concatenate(
        [jnp.broadcast_to(earlier[p : p + 1], (16, all_tokens)) for p in range(dp_count)], axis=0
    )
    r_iota = lax.broadcasted_iota(jnp.int32, shape, 0)
    slot = r_iota & 3
    quarter = (r_iota >> 2) & 3
    kept = jnp.where((rep_e == slot.astype(F32)) & (slot < capacity), rep_m, 0.0)
    for q in range(4):
        onehot_s[q] = jnp.where(quarter == q, kept, 0.0).astype(BF16)
    own_e = jnp.broadcast_to(earlier[dp_count : dp_count + 1], (8, all_tokens))
    own_g = jnp.broadcast_to(own_gate * own_hit, (8, all_tokens))
    sg_s[...] = jnp.broadcast_to(
        jnp.sum(
            jnp.where((own_e == row8.astype(F32)) & (row8 < capacity), own_g, 0.0),
            axis=1,
            keepdims=True,
        ),
        sg_s.shape,
    )

    ctx_s[...] = jnp.zeros_like(ctx_s)
    wg_s[pl.ds(model, wg_s.shape[0] - model), :] = jnp.zeros((wg_s.shape[0] - model, ff), BF16)
    wu_s[pl.ds(model, wu_s.shape[0] - model), :] = jnp.zeros((wu_s.shape[0] - model, ff), BF16)
    total_cols = tp_count * cols
    stg[:, pl.ds(total_cols, stg.shape[1] - total_cols)] = jnp.zeros(
        (all_tokens, stg.shape[1] - total_cols), F32
    )
    stg[:, pl.ds(0, total_cols)] = res_ref[...].astype(F32)
    lane = lax.broadcasted_iota(jnp.int32, (all_tokens, pad), 1)
    for j in range(tp_count):
        own_s[j] = jnp.where(lane < cols, stg[:, pl.ds(j * cols, pad)], 0.0)

    gain_rows = gain_ref.shape[0]
    gain_a[pl.ds(0, gain_rows), :] = gain_ref[...].astype(F32)
    gain_a[pl.ds(gain_rows, 8), :] = jnp.zeros((8, 128), F32)
    half = lax.broadcasted_iota(jnp.int32, (1, 128), 1) >= 64
    group = lax.broadcasted_iota(jnp.int32, (16, 128), 0) >> 2
    for src in range(peers):
        first, odd = divmod(src * cols, 128)
        block = jnp.zeros((16, 128), F32)
        for q in range(4):
            row = gain_a[pl.ds(first + q, 1), :]
            if odd:
                row = pltpu.roll(jnp.where(half, row, gain_a[pl.ds(first + q + 1, 1), :]), 64, 1)
            block = jnp.where(group == q, row, block)
        gain_s[src] = block

    q_copy.wait()
    c_copy.wait()
    for cp in vu_copies:
        cp.start()
    for cp in wo_copies:
        cp.start()
    wg_copy.start()
    wu_copy.start()

    score_scale = (VHEAD + ROPE) ** (-0.5)
    ctx_len = cache_s.shape[2]

    def token_step(i, carry):
        scores = jnp.dot(q_s[i], cache_s[i], preferred_element_type=F32) * score_scale
        live = lax.broadcasted_iota(jnp.int32, (heads, ctx_len), 1) < len_ref[i]
        scores = jnp.where(live, scores, -jnp.inf)
        top = jnp.max(scores, axis=1, keepdims=True)
        e = jnp.exp(scores - top)
        w = (e / jnp.sum(e, axis=1, keepdims=True)).astype(BF16)
        context = lax.dot_general(
            w,
            cache_s[i, pl.ds(0, LATENT), :],
            (((1,), (1,)), ((), ())),
            preferred_element_type=F32,
        )
        for k in range(LATENT // 128):
            ctx_s[k, pl.ds(i, heads, stride=rows_pad), :] = context[:, k * 128 : (k + 1) * 128]
        return carry

    lax.fori_loop(0, tokens, token_step, 0, unroll=UNROLL)

    def ag_copy(c, stage, right):
        return pltpu.make_async_remote_copy(
            src_ref=hbuf.at[c, d],
            dst_ref=hbuf.at[c, d],
            send_sem=ag_send.at[c, stage, 0 if right else 1],
            recv_sem=ag_recv.at[c, d],
            device_id=(g, d + stage + 1 if right else d - stage - 1, t),
            device_id_type=MESH,
        )

    def ag_each(c, stage, act):
        @pl.when(d + stage + 1 < dp_count)
        def _():
            act(ag_copy(c, stage, True), stage)

        @pl.when(d - stage - 1 >= 0)
        def _():
            act(ag_copy(c, stage, False), stage)

    def launch(copy, stage):
        copy.start()

    def last_arrival(c):
        for o in range(1, dp_count):
            src = lax.rem(d + o, dp_count)
            pltpu.make_async_remote_copy(
                src_ref=hbuf.at[c, src],
                dst_ref=hbuf.at[c, src],
                send_sem=ag_send.at[c, 0, 0],
                recv_sem=ag_recv.at[c, src],
                device_id=(g, src, t),
                device_id_type=MESH,
            ).wait_recv()

    for c in range(chunks):
        vu_copies[c].wait()
        for hl in range(hpc):
            h = c * hpc + hl
            rows = jnp.concatenate(
                [ctx_s[k, pl.ds(h * rows_pad, rows_pad), :] for k in range(LATENT // 128)], axis=1
            ).astype(BF16)
            out = jnp.dot(rows, vu_s[h], preferred_element_type=F32)
            pack_s[pl.ds(hl * tokens, tokens), :] = out[:tokens]
        hbuf[c, d] = pack_s[...].astype(BF16)
        if c == 0:
            pl.semaphore_wait(barrier, peers - 1)
        for stage in reversed(range(dp_count - 1)):
            ag_each(c, stage, launch)

    n_tile = 256
    n_count = wo_s.shape[1] // n_tile
    for c in range(chunks):
        wo_copies[c].wait()
        last_arrival(c)
        for src in range(dp_count):
            block = hbuf[c, src].astype(F32)
            for hl in range(hpc):
                lhs_s[pl.ds(src * tokens, tokens), pl.ds(hl * VHEAD, VHEAD)] = block[
                    hl * tokens : (hl + 1) * tokens
                ]
        left = lhs_s[...].astype(BF16)
        for n in range(n_count):
            sl = pl.ds(n * n_tile, n_tile)
            out = jnp.dot(left, wo_s[pl.ds(c * kc, kc), sl], preferred_element_type=F32)
            stg[:, sl] = out if c == 0 else stg[:, sl] + out

    for j in range(tp_count):
        piece = jnp.where(lane < cols, stg[:, pl.ds(j * cols, pad)], 0.0)
        red_send[j] = piece.astype(BF16)
        own_s[j] = own_s[j] + piece

    def rs_copy(o):
        peer = lax.rem(t + o, tp_count)
        return pltpu.make_async_remote_copy(
            src_ref=red_send.at[peer],
            dst_ref=red_recv.at[t],
            send_sem=rs_send.at[o],
            recv_sem=rs_recv.at[t],
            device_id=(g, d, peer),
            device_id_type=MESH,
        )

    def rs_arrival(o):
        src = lax.rem(t + o, tp_count)
        return pltpu.make_async_remote_copy(
            src_ref=red_send.at[src],
            dst_ref=red_recv.at[src],
            send_sem=rs_send.at[o],
            recv_sem=rs_recv.at[src],
            device_id=(g, d, src),
            device_id_type=MESH,
        )

    for o in range(1, tp_count):
        rs_copy(o).start()
    total = own_s[t]
    for o in range(1, tp_count):
        rs_arrival(o).wait_recv()
        total = total + red_recv[lax.rem(t + o, tp_count)].astype(F32)
    stream = total.astype(BF16)
    attn_ref[...] = stream[:, :cols]

    packed = jnp.zeros((16 * dp_count, 128), F32)
    for q in range(4):
        packed = packed + jnp.dot(
            onehot_s[q], stream[:, q * 128 : (q + 1) * 128], preferred_element_type=F32
        )
    packed = packed.astype(BF16)
    for p in range(dp_count):
        disp[p] = packed[p * 16 : (p + 1) * 16]

    def dx_copy(o):
        other = lax.rem(me + o, peers)
        return pltpu.make_async_remote_copy(
            src_ref=disp.at[other // tp_count],
            dst_ref=xrecv.at[me],
            send_sem=dx_send.at[o],
            recv_sem=dx_recv.at[me],
            device_id=(g, other // tp_count, lax.rem(other, tp_count)),
            device_id_type=MESH,
        )

    def dx_arrival(o):
        src = lax.rem(me + o, peers)
        return pltpu.make_async_remote_copy(
            src_ref=disp.at[0],
            dst_ref=xrecv.at[src],
            send_sem=dx_send.at[o],
            recv_sem=dx_recv.at[src],
            device_id=(g, src // tp_count, lax.rem(src, tp_count)),
            device_id_type=MESH,
        )

    for o in range(1, peers):
        dx_copy(o).start()
    xrecv[me] = disp[d]
    wg_copy.wait()
    wu_copy.wait()

    acc_g = jnp.zeros((16, ff), F32)
    acc_u = jnp.zeros((16, ff), F32)
    squares = jnp.zeros((16, 128), F32)

    def expert_piece(src, carry):
        acc_g, acc_u, squares = carry
        values = xrecv[src].astype(F32)
        scaled = values * gain_s[src]
        left = jnp.concatenate(
            [jnp.where(group == q, scaled, 0.0) for q in range(4)], axis=1
        ).astype(BF16)
        sl = pl.ds(pl.multiple_of(src * cols, 64), pad)
        acc_g = acc_g + jnp.dot(left, wg_s[sl, :], preferred_element_type=F32)
        acc_u = acc_u + jnp.dot(left, wu_s[sl, :], preferred_element_type=F32)
        return acc_g, acc_u, squares + values * values

    carry = expert_piece(me, (acc_g, acc_u, squares))

    def expert_step(o, carry):
        dx_arrival(o).wait_recv()
        return expert_piece(lax.rem(me + o, peers), carry)

    acc_g, acc_u, squares = lax.fori_loop(1, peers, expert_step, carry, unroll=True)

    def fold(a):
        return a[0:4] + a[4:8] + a[8:12] + a[12:16]

    mean_square = fold(jnp.sum(squares, axis=1, keepdims=True)) / model
    scale = lax.rsqrt(mean_square + 1e-06)
    gate_proj = fold(acc_g) * scale
    up_proj = fold(acc_u) * scale
    hidden = sg_s[0:4, 0:1] * (gate_proj / (1.0 + jnp.exp(-gate_proj))) * up_proj
    hid_ref[0] = hidden[0:capacity].astype(BF16)

    for c in range(chunks):
        for stage in range(dp_count - 1):
            ag_each(c, stage, lambda copy, stage: copy.wait_send())
    for o in range(1, tp_count):
        rs_copy(o).wait_send()
    for o in range(1, peers):
        dx_copy(o).wait_send()


UNROLL = 4


def fused_layer(
    queries,
    latent_cache,
    lengths,
    value_up,
    out_proj,
    residual,
    expert_ids,
    gate_weights,
    placement,
    norm_gain,
    w_gate,
    w_up,
):
    dp_count = lax.axis_size("dp")
    tp_count = lax.axis_size("tensor")
    all_tokens = expert_ids.shape[0]
    capacity = max(2, all_tokens * TOPK * 2 // EXPERTS)
    tokens, heads, width = queries.shape
    cols = residual.shape[1] // tp_count
    model = norm_gain.shape[0]
    ff = w_gate.shape[2]
    pad = 512
    chunks = 8
    rows_pad = 16
    peers = dp_count * tp_count
    hpc = heads // chunks
    hbm = pl.BlockSpec(memory_space=pl.ANY)
    vmem = pl.BlockSpec(memory_space=pltpu.VMEM)
    smem = pl.BlockSpec(memory_space=pltpu.SMEM)
    dma = pltpu.SemaphoreType.DMA
    return pl.pallas_call(
        functools.partial(layer_kernel, dp_count, tp_count),
        out_shape=(
            pltpu.VMEM((all_tokens, cols), BF16),
            pltpu.VMEM((1, capacity, ff), BF16),
        ),
        in_specs=[hbm, hbm, smem, hbm, hbm, vmem, vmem, vmem, vmem, vmem, hbm, hbm],
        out_specs=(vmem, vmem),
        scratch_shapes=[
            pltpu.VMEM((tokens, heads, width), BF16),
            pltpu.VMEM((tokens, width, latent_cache.shape[1]), BF16),
            pltpu.VMEM(value_up.shape, BF16),
            pltpu.VMEM(out_proj.shape, BF16),
            pltpu.VMEM((model + pad - cols, ff), BF16),
            pltpu.VMEM((model + pad - cols, ff), BF16),
            pltpu.VMEM((LATENT // 128, heads * rows_pad, 128), F32),
            pltpu.VMEM((chunks, dp_count, hpc * tokens, VHEAD), BF16),
            pltpu.VMEM((hpc * tokens, VHEAD), F32),
            pltpu.VMEM((dp_count * tokens, hpc * VHEAD), F32),
            pltpu.VMEM((model // 128 + 8, 128), F32),
            pltpu.VMEM((peers, 16, 128), F32),
            pltpu.VMEM((all_tokens, tp_count * cols + 128), F32),
            pltpu.VMEM((tp_count, all_tokens, pad), F32),
            pltpu.VMEM((tp_count, all_tokens, pad), BF16),
            pltpu.VMEM((tp_count, all_tokens, pad), BF16),
            pltpu.VMEM((4, 16 * dp_count, all_tokens), BF16),
            pltpu.VMEM((dp_count, 16, 128), BF16),
            pltpu.VMEM((peers, 16, 128), BF16),
            pltpu.VMEM((8, 128), F32),
            dma((2,)),
            dma((chunks,)),
            dma((chunks,)),
            dma((2,)),
            dma((chunks, dp_count, 2)),
            dma((chunks, dp_count)),
            dma((tp_count,)),
            dma((tp_count,)),
            dma((peers,)),
            dma((peers,)),
        ],
        compiler_params=pltpu.CompilerParams(
            collective_id=0, has_side_effects=True, vmem_limit_bytes=58 * 1024 * 1024
        ),
    )(
        queries,
        jnp.swapaxes(latent_cache, 1, 2),
        lengths,
        value_up,
        out_proj,
        residual,
        expert_ids.T,
        gate_weights.T,
        placement.reshape(1, -1),
        norm_gain.reshape(-1, 128),
        w_gate,
        w_up,
    )


def slot_table(expert_ids, placement, held_count, capacity):
    flat_ids = expert_ids.reshape(-1)
    id_match = flat_ids[:, None] == jnp.arange(EXPERTS, dtype=jnp.int32)[None, :]
    position = jnp.sum(jnp.where(id_match, placement[None, :], 0), axis=1)
    chosen = (position[:, None] == jnp.arange(held_count, dtype=jnp.int32)[None, :]).astype(
        jnp.int32
    )
    earlier = jnp.cumsum(chosen, axis=0) - chosen
    slot_index = jnp.sum(chosen * earlier, axis=1)
    kept_slot = (position < held_count) & (slot_index < capacity)
    target = jnp.where(kept_slot, position * capacity + slot_index, held_count * capacity)
    return target.reshape(expert_ids.shape)


def on_device(
    queries,
    latent_cache,
    lengths,
    value_up,
    out_proj,
    residual,
    expert_ids,
    gate_weights,
    placement,
    norm_gain,
    w_gate,
    w_up,
):
    dp_count = lax.axis_size("dp")
    tensor_count = lax.axis_size("tensor")
    token_count = expert_ids.shape[0]
    local_experts = w_gate.shape[0]
    held_count = local_experts * dp_count
    capacity = max(2, token_count * TOPK * 2 // EXPERTS)
    score_scale = (VHEAD + ROPE) ** (-0.5)
    scores = (
        jnp.einsum("thc,tsc->ths", queries, latent_cache, preferred_element_type=jnp.float32)
        * score_scale
    )
    live_keys = (
        jnp.arange(latent_cache.shape[1], dtype=jnp.int32)[None, None, :] < lengths[:, None, None]
    )
    scores = jnp.where(live_keys, scores, -jnp.inf)
    row_max = jnp.max(scores, axis=2, keepdims=True)
    exponent = jnp.exp(scores - row_max)
    attention_weights = (exponent / jnp.sum(exponent, axis=2, keepdims=True)).astype(jnp.bfloat16)
    context = jnp.einsum(
        "ths,tsc->thc",
        attention_weights,
        latent_cache[:, :, :LATENT],
        preferred_element_type=jnp.float32,
    ).astype(jnp.bfloat16)
    head_out = jnp.einsum(
        "thc,hcv->thv", context, value_up, preferred_element_type=jnp.float32
    ).astype(jnp.bfloat16)
    head_out = head_out.reshape(head_out.shape[0], -1)
    partial_sum = jnp.dot(
        lax.all_gather(head_out, "dp", axis=0, tiled=True),
        out_proj,
        preferred_element_type=jnp.float32,
    )
    target = slot_table(expert_ids, placement, held_count, capacity)
    slot_ids = jnp.arange(held_count * capacity, dtype=jnp.int32)
    slot_match = target[:, :, None] == slot_ids[None, None, :]
    onehot = jnp.any(slot_match, axis=1).astype(jnp.bfloat16)
    gate_all = jnp.sum(jnp.where(slot_match, gate_weights[:, :, None], 0.0), axis=(0, 1))
    owner_span = local_experts * capacity
    owner_index = lax.axis_index("dp")
    slot_gate = lax.dynamic_slice_in_dim(gate_all, owner_index * owner_span, owner_span).reshape(
        local_experts, capacity
    )
    gain_values = norm_gain.astype(jnp.float32)
    tensor_pos = lax.axis_index("tensor")
    summed_all = lax.psum(partial_sum, "tensor")
    stream_cols = (summed_all + residual.astype(jnp.float32)).astype(jnp.bfloat16)
    col_width = stream_cols.shape[1] // tensor_count
    attn_out = lax.dynamic_slice_in_dim(stream_cols, tensor_pos * col_width, col_width, 1)
    buffer = jnp.einsum(
        "td,tc->dc", onehot, stream_cols, preferred_element_type=jnp.float32
    ).astype(jnp.bfloat16)
    buffer = buffer.reshape(held_count, capacity, -1)
    values = lax.all_to_all(buffer, "dp", split_axis=0, concat_axis=2, tiled=True).astype(
        jnp.float32
    )
    mean_square = jnp.mean(values * values, axis=-1, keepdims=True)
    normed = (values * lax.rsqrt(mean_square + 1e-06) * gain_values).astype(jnp.bfloat16)
    gate_proj = jnp.einsum("end,edf->enf", normed, w_gate, preferred_element_type=jnp.float32)
    up_proj = jnp.einsum("end,edf->enf", normed, w_up, preferred_element_type=jnp.float32)
    hidden = jax.nn.silu(gate_proj) * up_proj
    result = (slot_gate[:, :, None] * hidden).astype(jnp.bfloat16)
    return (attn_out, result)


def solution(mesh):
    in_specs = (
        P(("groups", "dp"), "tensor", None),
        P(("groups", "dp"), None, None),
        P(("groups", "dp")),
        P("tensor", None, None),
        P("tensor", "dp"),
        P("groups", "dp"),
        P("groups", None),
        P("groups", None),
        P("groups"),
        P(),
        P("dp", None, "tensor"),
        P("dp", None, "tensor"),
    )
    out_specs = (P("groups", ("dp", "tensor")), P(("groups", "dp"), None, "tensor"))

    def layer(*args):
        token_count = args[6].shape[0]
        capacity = max(2, token_count * TOPK * 2 // EXPERTS)
        cols = args[5].shape[1] // mesh.shape["tensor"]
        fits = (
            args[10].shape[0] == 1
            and capacity <= 4
            and 384 < cols <= 512
            and cols % 64 == 0
            and args[5].shape[1] % 256 == 0
            and args[0].shape[0] <= 16
            and args[0].shape[1] % 8 == 0
            and mesh.shape["dp"] < 8
            and token_count % 16 == 0
            and args[0].shape[1] // 8 * args[0].shape[0] % 16 == 0
        )
        return (fused_layer if fits else on_device)(*args)

    return jax.shard_map(
        layer, mesh=mesh, in_specs=in_specs, out_specs=out_specs, check_vma=False
    )
```
